32 devices in a mesh: dp: 4 (over y, x), seq: 8 (over z, core).
Axes of the slice: x: 2, y: 2, z: 4, core: 2. Of those that a mesh axis runs over, the one named last changes fastest.
Arguments:
- queries: bfloat16 [32, 128, 4096], P(('dp', 'seq')), parts along dimension 0, may hold values from -6 to 6
- outputs: bfloat16 [32, 128, 4096], P(('dp', 'seq')), parts along dimension 0, may hold values from -3 to 3
- out_grads: bfloat16 [32, 128, 4096], P(('dp', 'seq')), parts along dimension 0, may hold values from -12 to 12
- resp_keys: bfloat16 [32, 128, 512], P(('dp', 'seq')), parts along dimension 0, may hold values from -6 to 6
- resp_values: bfloat16 [32, 128, 512], P(('dp', 'seq')), parts along dimension 0, may hold values from -6 to 6
- lengths: int32 [32], P('dp'), parts along dimension 0, may hold values from 1 to 128, 512 in all
- prompt_keys: bfloat16 [1536, 512], P(('dp', 'seq')), parts along dimension 0, may hold values from -6 to 6
- prompt_values: bfloat16 [1536, 512], P(('dp', 'seq')), parts along dimension 0, may hold values from -6 to 6
Outputs:
- query_grads: bfloat16 [32, 128, 4096], P(('dp', 'seq')), parts along dimension 0
- resp_key_grads: bfloat16 [32, 128, 512], P(('dp', 'seq')), parts along dimension 0
- resp_value_grads: bfloat16 [32, 128, 512], P(('dp', 'seq')), parts along dimension 0
- prompt_key_grads: bfloat16 [1536, 512], P(('dp', 'seq')), parts along dimension 0
- prompt_value_grads: bfloat16 [1536, 512], P(('dp', 'seq')), parts along dimension 0
The draws below stay inside these ranges and needn't reach their ends.
There are 4 independent parts, one for each index of `dp`. The reference program is written for one: setup_inputs(seed, part) draws one part's arguments, and reference() takes and returns one part's arrays. A program takes and returns all parts, laid end to end along the dimension named above; each array names one. Nothing has to cross between parts.
All inputs are finite; a program needn't handle non-finite values.
Results may differ from the reference program's by a relative error of at most 0.0055.
Values may be sent and summed in bfloat16 or wider, within the bound.
No kernel may reach another device: no remote copies, remote signals or barrier semaphores. Data moves between devices by JAX's collectives and lax.ppermute only.
A program may use at most 64 MiB of HBM per device.

```python
import math
import jax
import jax.numpy as jnp
import numpy as np
from jax import lax

HEADS = 32
KV_HEADS = 4
HEAD_DIM = 128
RESP_LEN = 128
PROMPT = 384
RESPONSES = 8


def draw_queries(key, part):
    key = jax.random.fold_in(key, 3)
    drawn = jnp.clip(jax.random.normal(key, (RESPONSES, RESP_LEN, HEADS, HEAD_DIM), jnp.float32), -4.0, 4.0)
    return drawn.reshape(RESPONSES, RESP_LEN, HEADS * HEAD_DIM).astype(jnp.bfloat16)


def draw_prompt_keys(key, part):
    key = jax.random.fold_in(key, 5)
    drawn = jnp.clip(jax.random.normal(key, (PROMPT, KV_HEADS * HEAD_DIM), jnp.float32), -4.0, 4.0)
    return drawn.astype(jnp.bfloat16)


def block_scale(rng, dims, shards, least, high):
    level, own = 1.0, jax.random.fold_in(rng, 6)
    for dim, shards_of in shards:
        draws = jnp.exp(jax.random.uniform(jax.random.fold_in(own, dim), (shards_of,), jnp.float32, least / len(shards), high / len(shards)))
        level = level * jnp.repeat(draws, dims[dim] // shards_of).reshape([-1 if axis == dim else 1 for axis in range(len(dims))])
    return level


def profile(number_of, total, limit, slope):
    portions = [(1 << 20) // math.isqrt(standing ** slope) + 1 for standing in range(2, number_of + 1)]
    surplus, counts = total - limit - (number_of - 1), [1] * (number_of - 1)
    while surplus > 0:
        movable = [i for i in range(number_of - 1) if counts[i] < limit]
        pool, left = sum([portions[i] for i in movable]), surplus
        for i in movable:
            extra = min(limit - counts[i], max(1, left * portions[i] // pool), surplus)
            counts[i] = counts[i] + extra
            surplus = surplus - extra
    return np.array([limit] + counts)


def ragged_sizes(rng, amount, total, limit, skew):
    if amount == 2:
        one = jax.random.randint(rng, (), max(1, total - limit), min(limit, total - 1) + 1)
        return jnp.stack([one, total - one])
    sizes = jnp.asarray(profile(amount, total, limit, skew), jnp.int32)
    pairs = (amount - 1) // 2
    giver, taker = sizes[1:1 + 2 * pairs:2], sizes[2:2 + 2 * pairs:2]
    room = jnp.minimum(giver - 1, limit - taker)
    moved = jax.random.randint(jax.random.fold_in(rng, 1), (pairs,), 0, 1 << 20) % (room + 1)
    sizes = sizes.at[1:1 + 2 * pairs:2].set(giver - moved).at[2:2 + 2 * pairs:2].set(taker + moved)
    return sizes[jax.random.permutation(jax.random.fold_in(rng, 2), amount)]


def centred(stream_key, dims, deviation, limit, cuts=(), held_as=jnp.bfloat16):
    loudness = block_scale(stream_key, dims, cuts, -0.22, 0.18) if cuts else 1.0
    values = jax.random.normal(stream_key, dims, jnp.float32) * deviation * loudness
    return jnp.minimum(jnp.maximum(values, -limit), limit).astype(held_as)


def setup_inputs(seed: int = 0, part: int = 0) -> dict:
    key_of = jax.random.split(jax.random.key(seed), 9)
    part_splits = jax.random.split(jax.random.fold_in(key_of[8], part), 9)
    return {
        "queries": draw_queries(jax.random.fold_in(jax.random.fold_in(key_of[8], part), 71), part),
        "outputs": centred(part_splits[1], (RESPONSES, RESP_LEN, HEADS * HEAD_DIM), 0.5, 3.0, ((0, 8),)),
        "out_grads": centred(part_splits[2], (RESPONSES, RESP_LEN, HEADS * HEAD_DIM), 2.0, 12.0, ((0, 8),)),
        "resp_keys": centred(part_splits[3], (RESPONSES, RESP_LEN, KV_HEADS * HEAD_DIM), 1.0, 6.0, ((0, 8),)),
        "resp_values": centred(part_splits[4], (RESPONSES, RESP_LEN, KV_HEADS * HEAD_DIM), 1.0, 6.0, ((0, 8),)),
        "lengths": ragged_sizes(part_splits[5], RESPONSES, RESPONSES * RESP_LEN // 2, RESP_LEN, 2).astype(jnp.int32),
        "prompt_keys": draw_prompt_keys(jax.random.fold_in(jax.random.fold_in(key_of[8], part), 71), part),
        "prompt_values": centred(part_splits[7], (PROMPT, KV_HEADS * HEAD_DIM), 1.0, 6.0, ((0, 8),)),
    }


def group_grads(query_rows, output_rows, grad_rows, key_block, value_block, length):
    softmax_scale = HEAD_DIM ** -0.5
    position = lax.iota(jnp.int32, RESP_LEN)
    key_position = lax.iota(jnp.int32, PROMPT + RESP_LEN)
    visible = (key_position[None, :] < PROMPT) | (key_position[None, :] - PROMPT <= position[:, None])
    live_rows = position < length
    scores = jnp.einsum("tgd,jd->gtj", query_rows.astype(jnp.float32), key_block.astype(jnp.float32)) * softmax_scale
    top_score = jnp.max(jnp.where(visible[None], scores, -1e30), axis=2)
    exp_total = jnp.sum(jnp.where(visible[None], jnp.exp(scores - top_score[:, :, None]), 0.0), axis=2)
    log_total = top_score + jnp.log(exp_total)
    usable = (visible & live_rows[:, None])[None]
    probability = jnp.where(usable, jnp.exp(scores - log_total[:, :, None]), 0.0)
    row_delta = jnp.sum(grad_rows.astype(jnp.float32) * output_rows.astype(jnp.float32), axis=2).T
    prob_grad = jnp.einsum("tgd,jd->gtj", grad_rows.astype(jnp.float32), value_block.astype(jnp.float32))
    score_grad = (probability * (prob_grad - row_delta[:, :, None])).astype(jnp.bfloat16)
    weights = probability.astype(jnp.bfloat16)
    value_grad = jnp.einsum("gtj,tgd->jd", weights.astype(jnp.float32), grad_rows.astype(jnp.float32))
    key_grad = jnp.einsum("gtj,tgd->jd", score_grad.astype(jnp.float32), query_rows.astype(jnp.float32)) * softmax_scale
    query_grad = jnp.einsum("gtj,jd->tgd", score_grad.astype(jnp.float32), key_block.astype(jnp.float32)) * softmax_scale
    return query_grad, key_grad, value_grad


def one_response(query_all, output_all, grad_all, resp_key_rows, resp_value_rows, length, prompt_keys, prompt_values):
    per_group = HEADS // KV_HEADS
    width = per_group * HEAD_DIM
    query_parts = []
    resp_key_parts = []
    resp_value_parts = []
    prompt_key_parts = []
    prompt_value_parts = []
    for group_index in range(KV_HEADS):
        low = group_index * width
        query_rows = query_all[:, low:low + width].reshape(RESP_LEN, per_group, HEAD_DIM)
        output_rows = output_all[:, low:low + width].reshape(RESP_LEN, per_group, HEAD_DIM)
        grad_rows = grad_all[:, low:low + width].reshape(RESP_LEN, per_group, HEAD_DIM)
        column = group_index * HEAD_DIM
        key_block = jnp.concatenate([prompt_keys[:, column:column + HEAD_DIM], resp_key_rows[:, column:column + HEAD_DIM]], axis=0)
        value_block = jnp.concatenate([prompt_values[:, column:column + HEAD_DIM], resp_value_rows[:, column:column + HEAD_DIM]], axis=0)
        query_grad, key_grad, value_grad = group_grads(query_rows, output_rows, grad_rows, key_block, value_block, length)
        query_parts.append(query_grad.reshape(RESP_LEN, width))
        prompt_key_parts.append(key_grad[:PROMPT])
        resp_key_parts.append(key_grad[PROMPT:])
        prompt_value_parts.append(value_grad[:PROMPT])
        resp_value_parts.append(value_grad[PROMPT:])
    return (jnp.concatenate(query_parts, axis=1).astype(jnp.bfloat16),
            jnp.concatenate(resp_key_parts, axis=1).astype(jnp.bfloat16),
            jnp.concatenate(resp_value_parts, axis=1).astype(jnp.bfloat16),
            jnp.concatenate(prompt_key_parts, axis=1),
            jnp.concatenate(prompt_value_parts, axis=1))


def reference(queries, outputs, out_grads, resp_keys, resp_values, lengths, prompt_keys, prompt_values):
    def accumulate(running, response):
        query_all, output_all, grad_all, key_rows, value_rows, length = response
        query_grad, key_grad, value_grad, prompt_key_part, prompt_value_part = one_response(
            query_all, output_all, grad_all, key_rows, value_rows, length, prompt_keys, prompt_values)
        return (running[0] + prompt_key_part, running[1] + prompt_value_part), (query_grad, key_grad, value_grad)

    zero_sum = jnp.zeros((PROMPT, KV_HEADS * HEAD_DIM), jnp.float32)
    (key_sum, value_sum), (query_grads, resp_key_grads, resp_value_grads) = lax.scan(
        accumulate, (zero_sum, zero_sum), (queries, outputs, out_grads, resp_keys, resp_values, lengths))
    return query_grads, resp_key_grads, resp_value_grads, key_sum.astype(jnp.bfloat16), value_sum.astype(jnp.bfloat16)
```

```python
import functools

import jax
import jax.numpy as jnp
from jax import lax
from jax.experimental import pallas as pl
from jax.experimental.pallas import tpu as pltpu
from jax.sharding import PartitionSpec as P

HEAD_DIM = 128
SCALE = HEAD_DIM ** (-0.5)
LOG2E = 1.4426950408889634
NT = (((1,), (1,)), ((), ()))
CORES = 2
CHUNK = 32
DELTA_TERMS = 3
BF16 = jnp.bfloat16
F32 = jnp.float32
VMEM_SPEC = pl.BlockSpec(memory_space=pltpu.VMEM)
HBM_SPEC = pl.BlockSpec(memory_space=pltpu.HBM)
SMEM_SPEC = pl.BlockSpec(memory_space=pltpu.SMEM)
MIB = 1024 * 1024
PARAMS = pltpu.CompilerParams(vmem_limit_bytes=24 * MIB)


def shape(*dims):
    return jax.ShapeDtypeStruct(dims, BF16)


def dot(a, b, dims=None):
    if dims is None:
        return jnp.dot(a, b, preferred_element_type=F32)
    return lax.dot_general(a, b, dims, preferred_element_type=F32)


def head_slice(index):
    return slice(index * HEAD_DIM, (index + 1) * HEAD_DIM)


def prepare_kernel(groups, len_ref, *refs):
    wide_in, narrow_in, refs = refs[:3], refs[3:5], refs[5:]
    (q_rows, g_rows, q_cols, g_cols, live_ref), narrow_out, refs = refs[:5], refs[5:7], refs[7:]
    wide_buf, (wide_sem, narrow_sem) = refs[:3], refs[3:]
    rows = wide_buf[0].shape[0]
    width = wide_buf[0].shape[1] // groups
    wide = [
        [
            pltpu.make_async_copy(src.at[:, group * width : (group + 1) * width], buf.at[:, group * width : (group + 1) * width], wide_sem.at[group, i])
            for i, (src, buf) in enumerate(zip(wide_in, wide_buf))
        ]
        for group in range(groups)
    ]
    narrow = [pltpu.make_async_copy(src, out, narrow_sem.at[i]) for i, (src, out) in enumerate(zip(narrow_in, narrow_out))]
    for copy in sum(wide, []) + narrow:
        copy.start()
    length = len_ref[lax.axis_index("seq")]
    live_ref[...] = jnp.where(lax.broadcasted_iota(jnp.int32, live_ref.shape, 0) < length, 1.0, 0.0)
    lane = lax.broadcasted_iota(jnp.int32, (rows, HEAD_DIM), 1)
    q_ref, o_ref, g_ref = wide_buf
    heads = width // HEAD_DIM
    for head in range(groups * heads):
        if head % heads == 0:
            for copy in wide[head // heads]:
                copy.wait()
        cols = head_slice(head)
        span = slice(head * rows, (head + 1) * rows)
        q = q_ref[:, cols]
        g = g_ref[:, cols]
        left = jnp.sum(g.astype(F32) * o_ref[:, cols].astype(F32), axis=1, keepdims=True)
        terms = jnp.zeros((rows, HEAD_DIM), F32)
        for term in range(DELTA_TERMS):
            rounded = left.astype(BF16).astype(F32)
            terms = jnp.where(lane == term, rounded, terms)
            left = left - rounded
        q_rows[span, :] = q
        g_rows[span, :HEAD_DIM] = g
        g_rows[span, HEAD_DIM:] = terms.astype(BF16)
        q_cols[:, span] = q.T
        g_cols[:, span] = g.T
    for copy in narrow:
        copy.wait()


def prepare(lengths, q, o, g, rk, rv):
    rows, width = q.shape
    groups = rk.shape[1] // HEAD_DIM
    flat = rows * width // HEAD_DIM
    narrow = [rk, rv]
    return pl.pallas_call(
        functools.partial(prepare_kernel, groups),
        in_specs=[SMEM_SPEC] + [HBM_SPEC] * 5,
        out_specs=[VMEM_SPEC] * 7,
        out_shape=[
            shape(flat, HEAD_DIM),
            shape(flat, 2 * HEAD_DIM),
            shape(HEAD_DIM, flat),
            shape(HEAD_DIM, flat),
            jax.ShapeDtypeStruct((rows, HEAD_DIM), F32),
        ]
        + [shape(*x.shape) for x in narrow],
        scratch_shapes=[pltpu.VMEM((rows, width), BF16)] * 3
        + [pltpu.SemaphoreType.DMA((groups, 3)), pltpu.SemaphoreType.DMA((2,))],
        compiler_params=PARAMS,
        cost_estimate=pl.CostEstimate(flops=rows * width * 4000, bytes_accessed=16 * rows * width, transcendentals=0),
    )(lengths, *[pltpu.with_memory_space_constraint(x, pltpu.HBM) for x in [q, o, g] + narrow])


def attention_kernel(chips, piece_rows, live_ref, q_rows, g_rows, q_cols, g_cols, rk_ref, rv_ref, *rest):
    pieces = CORES * chips
    kv_refs, (dq_ref, drk_ref, drv_ref), rest = rest[:pieces], rest[pieces : pieces + 3], rest[pieces + 3 :]
    d_own, d_other, (k_buf, v_buf, s_buf, dp_buf, p_buf, ds_buf) = rest[:chips], rest[chips], rest[chips + 1 :]
    rows, width = rk_ref.shape
    groups = width // HEAD_DIM
    flat = q_rows.shape[0] // groups
    block = flat // 2
    keys = k_buf.shape[1]
    prompt = keys - rows
    diagonal = lax.broadcasted_iota(jnp.int32, (CHUNK, rows), 1) - lax.broadcasted_iota(jnp.int32, (CHUNK, rows), 0)
    minus = jnp.where(lax.broadcasted_iota(jnp.int32, (keys, HEAD_DIM), 1) < DELTA_TERMS, -1.0, 0.0).astype(BF16)

    def load_keys(group):
        k_cols = head_slice(group)
        v_cols = slice(width + group * HEAD_DIM, width + (group + 1) * HEAD_DIM)
        for i in range(pieces):
            span = slice(i * piece_rows, (i + 1) * piece_rows)
            k_buf[group, span, :] = kv_refs[i][:, k_cols]
            v_buf[group, span, :HEAD_DIM] = kv_refs[i][:, v_cols]
        k_buf[group, prompt:, :] = rk_ref[:, k_cols]
        v_buf[group, prompt:, :HEAD_DIM] = rv_ref[:, k_cols]
        v_buf[group, :, HEAD_DIM:] = minus

    def scores(half):
        group, slot = half // 2, half % 2
        if slot == 0:
            load_keys(group)
        span = slice(half * block, (half + 1) * block)
        s_buf[slot] = dot(q_rows[span, :], k_buf[group], NT)
        dp_buf[slot] = dot(g_rows[span, :], v_buf[group], NT)

    def soften(half):
        slot = half % 2
        for low in range(0, block, CHUNK):
            first = low % rows
            span = slice(low, low + CHUNK)
            s = s_buf[slot, span, :]
            s = jnp.concatenate([s[:, :prompt], jnp.where(diagonal > first, -1e30, s[:, prompt:])], axis=1)
            top = jnp.max(s, axis=1, keepdims=True)
            e = jnp.exp2((s - top) * (SCALE * LOG2E))
            weight = (1.0 / jnp.sum(e, axis=1, keepdims=True)) * live_ref[first : first + CHUNK, :]
            p = e * jnp.concatenate([weight] * (keys // HEAD_DIM), axis=1)
            p_buf[slot, span, :] = p.astype(BF16)
            ds_buf[slot, span, :] = (p * dp_buf[slot, span, :]).astype(BF16)

    def gradients(half):
        group, slot = half // 2, half % 2
        span = slice(half * block, (half + 1) * block)
        dq = (dot(ds_buf[slot], k_buf[group]) * SCALE).astype(BF16)
        for i in range(block // rows):
            dq_ref[:, head_slice(half * (block // rows) + i)] = dq[i * rows : (i + 1) * rows]
        return dot(q_cols[:, span], ds_buf[slot]), dot(g_cols[:, span], p_buf[slot])

    scores(0)
    held = None
    for half in range(2 * groups):
        if half + 1 < 2 * groups:
            scores(half + 1)
        soften(half)
        dk, dv = gradients(half)
        if half % 2 == 0:
            held = (dk, dv)
            continue
        group = half // 2
        dk = ((held[0] + dk) * SCALE).T
        dv = (held[1] + dv).T
        for grad, low in ((dk, 0), (dv, width)):
            cols = slice(low + group * HEAD_DIM, low + (group + 1) * HEAD_DIM)
            for i in range(chips):
                d_own[i][:, cols] = grad[i * piece_rows : (i + 1) * piece_rows]
                d_other[i, :, cols] = grad[(chips + i) * piece_rows : (chips + i + 1) * piece_rows].astype(BF16)
        drk_ref[:, head_slice(group)] = dk[prompt:].astype(BF16)
        drv_ref[:, head_slice(group)] = dv[prompt:].astype(BF16)


def attention(prepared, kv_pieces):
    live, q_rows, g_rows, q_cols, g_cols, rk, rv = prepared
    rows, kv_width = rk.shape
    groups = kv_width // HEAD_DIM
    flat = q_rows.shape[0]
    pieces = len(kv_pieces)
    chips = pieces // CORES
    piece_rows = kv_pieces[0].shape[0]
    keys = pieces * piece_rows + rows
    block = flat // groups // 2
    return pl.pallas_call(
        functools.partial(attention_kernel, chips, piece_rows),
        in_specs=[VMEM_SPEC] * (7 + pieces),
        out_specs=[VMEM_SPEC] * (4 + chips),
        out_shape=[shape(rows, flat // rows * HEAD_DIM), shape(rows, kv_width), shape(rows, kv_width)]
        + [jax.ShapeDtypeStruct((piece_rows, 2 * kv_width), F32)] * chips
        + [shape(chips, piece_rows, 2 * kv_width)],
        scratch_shapes=[
            pltpu.VMEM((groups, keys, HEAD_DIM), BF16),
            pltpu.VMEM((groups, keys, 2 * HEAD_DIM), BF16),
            pltpu.VMEM((2, block, keys), F32),
            pltpu.VMEM((2, block, keys), F32),
            pltpu.VMEM((2, block, keys), BF16),
            pltpu.VMEM((2, block, keys), BF16),
        ],
        compiler_params=PARAMS,
        cost_estimate=pl.CostEstimate(
            flops=10 * flat * keys * HEAD_DIM, bytes_accessed=10 * flat * HEAD_DIM, transcendentals=flat * keys
        ),
    )(live, q_rows, g_rows, q_cols, g_cols, rk, rv, *kv_pieces)


def to_chip(x, chips, step):
    if chips & (chips - 1) == 0:
        route = [chip ^ step for chip in range(chips)]
    else:
        route = [(step - chip) % chips for chip in range(chips)]
    pairs = [(CORES * chip + core, CORES * route[chip] + core) for chip in range(chips) for core in range(CORES)]
    return lax.ppermute(x, "seq", pairs)


def swap_core(x, chips):
    pairs = [(CORES * chip + core, CORES * chip + 1 - core) for chip in range(chips) for core in range(CORES)]
    return lax.ppermute(x, "seq", pairs)


def local(chips, queries, outputs, out_grads, resp_keys, resp_values, lengths, prompt_keys, prompt_values):
    kv_width = prompt_keys.shape[1]
    steps = [1] + list(range(chips - 1, 1, -1))
    kv = jnp.concatenate([prompt_keys, prompt_values], axis=1)
    far = [to_chip(kv, chips, step) for step in steps]
    prepared = prepare(lengths, queries[0], outputs[0], out_grads[0], resp_keys[0], resp_values[0])
    far, prepared = lax.optimization_barrier((far, prepared))
    q_rows, g_rows, q_cols, g_cols, live, rk, rv = prepared
    own = [kv] + far
    other = [swap_core(x, chips) for x in own]
    results = attention((live, q_rows, g_rows, q_cols, g_cols, rk, rv), own + other)
    dq, drk, drv = results[:3]
    swapped = swap_core(results[3 + chips], chips)
    both = [results[3 + i] + swapped[i].astype(F32) for i in range(chips)]
    back = [to_chip(both[1 + steps.index(step)].astype(BF16), chips, step) for step in [2, 1] + list(range(3, chips))]
    total = sum([x.astype(F32) for x in back], both[0]).astype(BF16)
    return dq[None], drk[None], drv[None], total[:, :kv_width], total[:, kv_width:]


def solution(mesh):
    chips = mesh.shape["seq"] // CORES
    split = ("dp", "seq")
    row3 = P(split, None, None)
    row2 = P(split, None)
    return jax.shard_map(
        functools.partial(local, chips),
        mesh=mesh,
        in_specs=(row3, row3, row3, row3, row3, P("dp"), row2, row2),
        out_specs=(row3, row3, row3, row2, row2),
        check_vma=False,
    )
```

```python
import functools

import jax
import jax.numpy as jnp
from jax import lax
from jax.experimental import pallas as pl
from jax.experimental.pallas import tpu as pltpu
from jax.sharding import PartitionSpec as P

HEAD_DIM = 128
SCALE = HEAD_DIM ** (-0.5)
LOG2E = 1.4426950408889634
NT = (((1,), (1,)), ((), ()))
CORES = 2
CHUNK = 32
DELTA_TERMS = 2
BF16 = jnp.bfloat16
F32 = jnp.float32
VMEM_SPEC = pl.BlockSpec(memory_space=pltpu.VMEM)
HBM_SPEC = pl.BlockSpec(memory_space=pltpu.HBM)
SMEM_SPEC = pl.BlockSpec(memory_space=pltpu.SMEM)
MIB = 1024 * 1024
PARAMS = pltpu.CompilerParams(vmem_limit_bytes=24 * MIB)


def shape(*dims):
    return jax.ShapeDtypeStruct(dims, BF16)


def dot(a, b, dims=None):
    if dims is None:
        return jnp.dot(a, b, preferred_element_type=F32)
    return lax.dot_general(a, b, dims, preferred_element_type=F32)


def head_slice(index):
    return slice(index * HEAD_DIM, (index + 1) * HEAD_DIM)


def in_hbm(*arrays):
    return [pltpu.with_memory_space_constraint(x, pltpu.HBM) for x in arrays]


def prepare_kernel(groups, len_ref, *refs):
    wide_in, narrow_in, refs = refs[:3], refs[3:5], refs[5:]
    (q_rows, g_rows, q_cols, g_cols, live_ref), narrow_out, refs = refs[:5], refs[5:7], refs[7:]
    wide_buf, (wide_sem, narrow_sem) = refs[:3], refs[3:]
    rows = wide_buf[0].shape[0]
    width = wide_buf[0].shape[1] // groups
    wide = [
        [
            pltpu.make_async_copy(src.at[:, group * width : (group + 1) * width], buf.at[:, group * width : (group + 1) * width], wide_sem.at[group, i])
            for i, (src, buf) in enumerate(zip(wide_in, wide_buf))
        ]
        for group in range(groups)
    ]
    narrow = [pltpu.make_async_copy(src, out, narrow_sem.at[i]) for i, (src, out) in enumerate(zip(narrow_in, narrow_out))]
    for copy in sum(wide, []) + narrow:
        copy.start()
    length = len_ref[lax.axis_index("seq")]
    live_ref[...] = jnp.where(lax.broadcasted_iota(jnp.int32, live_ref.shape, 0) < length, 1.0, 0.0)
    lane = lax.broadcasted_iota(jnp.int32, (rows, HEAD_DIM), 1)
    square = (HEAD_DIM, HEAD_DIM)
    same = lax.broadcasted_iota(jnp.int32, square, 0) == lax.broadcasted_iota(jnp.int32, square, 1)
    identity = jnp.where(same, 1.0, 0.0).astype(BF16)
    ones = jnp.ones((2 * HEAD_DIM, HEAD_DIM), BF16)
    q_ref, o_ref, g_ref = wide_buf
    heads = width // HEAD_DIM
    for group in range(groups):
        for copy in wide[group]:
            copy.wait()
        for head in range(group * heads, (group + 1) * heads):
            cols = head_slice(head)
            span = slice(head * rows, (head + 1) * rows)
            g = g_ref[:, cols]
            product = g.astype(F32) * o_ref[:, cols].astype(F32)
            high = product.astype(BF16)
            low = (product - high.astype(F32)).astype(BF16)
            left = dot(jnp.concatenate([high, low], axis=1), ones)
            terms = jnp.zeros((rows, HEAD_DIM), F32)
            for term in range(DELTA_TERMS):
                rounded = left.astype(BF16).astype(F32)
                terms = jnp.where(lane == term, rounded, terms)
                left = left - rounded
            q_rows[span, :] = q_ref[:, cols]
            g_rows[span, :HEAD_DIM] = g
            g_rows[span, HEAD_DIM:] = terms.astype(BF16)
        span = slice(group * heads * rows, (group + 1) * heads * rows)
        q_cols[:, span] = dot(identity, q_rows[span, :], NT).astype(BF16)
        g_cols[:, span] = dot(identity, g_rows[span, :HEAD_DIM], NT).astype(BF16)
    for copy in narrow:
        copy.wait()


def prepare(lengths, q, o, g, rk, rv):
    rows, width = q.shape
    groups = rk.shape[1] // HEAD_DIM
    flat = rows * width // HEAD_DIM
    narrow = [rk, rv]
    return pl.pallas_call(
        functools.partial(prepare_kernel, groups),
        in_specs=[SMEM_SPEC] + [HBM_SPEC] * 5,
        out_specs=[VMEM_SPEC] * 7,
        out_shape=[
            shape(flat, HEAD_DIM),
            shape(flat, 2 * HEAD_DIM),
            shape(HEAD_DIM, flat),
            shape(HEAD_DIM, flat),
            jax.ShapeDtypeStruct((rows, HEAD_DIM), F32),
        ]
        + [shape(*x.shape) for x in narrow],
        scratch_shapes=[pltpu.VMEM((rows, width), BF16)] * 3
        + [pltpu.SemaphoreType.DMA((groups, 3)), pltpu.SemaphoreType.DMA((2,))],
        compiler_params=PARAMS,
        cost_estimate=pl.CostEstimate(flops=rows * width * 4000, bytes_accessed=16 * rows * width, transcendentals=0),
    )(lengths, *in_hbm(q, o, g, *narrow))


def read_pieces(joined, refs):
    k_refs, v_refs = [], []
    for both in joined:
        k_refs.append(refs[0].at[0] if both else refs[0])
        v_refs.append(refs[0].at[1] if both else refs[1])
        refs = refs[1 if both else 2 :]
    return k_refs, v_refs, refs


def attention_kernel(chips, piece_rows, joined, live_ref, q_rows, g_rows, q_cols, g_cols, rk_ref, rv_ref, *rest):
    pieces = CORES * chips
    k_refs, v_refs, rest = read_pieces(joined, rest)
    whole, rest = rest[:3], rest[3:]
    d_own, d_other, rest = rest[:chips], rest[chips : 2 * chips], rest[2 * chips :]
    k_buf, v_buf, s_buf, dp_buf, p_buf, ds_buf, dq_buf, drk_buf, drv_buf, sem = rest
    rows, width = rk_ref.shape
    groups = width // HEAD_DIM
    block = q_rows.shape[0] // groups // 2
    per_half = block // rows
    keys = k_buf.shape[1]
    prompt = keys - rows
    diagonal = lax.broadcasted_iota(jnp.int32, (CHUNK, rows), 1) - lax.broadcasted_iota(jnp.int32, (CHUNK, rows), 0)
    minus = jnp.where(lax.broadcasted_iota(jnp.int32, (keys, HEAD_DIM), 1) < DELTA_TERMS, -1.0, 0.0).astype(BF16)

    def place(half):
        return slice(half * block, (half + 1) * block)

    def load_keys(group):
        cols = head_slice(group)
        for i in range(pieces):
            span = slice(i * piece_rows, (i + 1) * piece_rows)
            k_buf[group, span, :] = k_refs[i][:, cols]
            v_buf[group, span, :HEAD_DIM] = v_refs[i][:, cols]
        k_buf[group, prompt:, :] = rk_ref[:, cols]
        v_buf[group, prompt:, :HEAD_DIM] = rv_ref[:, cols]
        v_buf[group, :, HEAD_DIM:] = minus

    def scores(half):
        s_buf[half % 2] = dot(q_rows[place(half), :], k_buf[half // 2], NT)

    def prob_grads(half):
        dp_buf[half % 2] = dot(g_rows[place(half), :], v_buf[half // 2], NT)

    def soften(half, low):
        slot = half % 2
        first = low % rows
        span = slice(low, low + CHUNK)
        s = s_buf[slot, span, :]
        s = jnp.concatenate([s[:, :prompt], jnp.where(diagonal > first, -1e30, s[:, prompt:])], axis=1)
        e = jnp.exp2((s - jnp.max(s, axis=1, keepdims=True)) * (SCALE * LOG2E))
        weight = (1.0 / jnp.sum(e, axis=1, keepdims=True)) * live_ref[first : first + CHUNK, :]
        p = e * jnp.concatenate([weight] * (keys // HEAD_DIM), axis=1)
        p_buf[slot, span, :] = p.astype(BF16)
        ds_buf[slot, span, :] = (p * dp_buf[slot, span, :]).astype(BF16)

    def query_grads(half):
        dq = (dot(ds_buf[half % 2], k_buf[half // 2]) * SCALE).astype(BF16)
        for i in range(per_half):
            dq_buf[:, head_slice(half * per_half + i)] = dq[i * rows : (i + 1) * rows]

    sums = {}

    def key_grads(half):
        sums["k", half] = dot(q_cols[:, place(half)], ds_buf[half % 2])

    def value_grads(half):
        sums["v", half] = dot(g_cols[:, place(half)], p_buf[half % 2])

    def finish(group):
        cols = head_slice(group)
        dk = ((sums["k", 2 * group] + sums["k", 2 * group + 1]) * SCALE).T
        dv = (sums["v", 2 * group] + sums["v", 2 * group + 1]).T
        for kind, grad in enumerate((dk, dv)):
            for i in range(chips):
                d_own[i][kind, :, cols] = grad[i * piece_rows : (i + 1) * piece_rows]
                d_other[i][kind, :, cols] = grad[(chips + i) * piece_rows : (chips + i + 1) * piece_rows].astype(BF16)
        drk_buf[:, cols] = dk[prompt:].astype(BF16)
        drv_buf[:, cols] = dv[prompt:].astype(BF16)
        copies = []
        for i, (buf, out) in enumerate(zip((dq_buf, drk_buf, drv_buf), whole)):
            step = buf.shape[1] // groups
            part = slice(group * step, (group + 1) * step)
            copies.append(pltpu.make_async_copy(buf.at[:, part], out.at[:, part], sem.at[group, i]))
            copies[-1].start()
        return copies

    halves = 2 * groups
    chunks = range(0, block, CHUNK)
    load_keys(0)
    scores(0)
    prob_grads(0)
    stores = []
    for half in range(halves + 1):
        tasks = []
        if half + 1 < halves:
            if (half + 1) % 2 == 0:
                load_keys((half + 1) // 2)
            tasks += [functools.partial(task, half + 1) for task in (scores, prob_grads)]
        if half:
            tasks += [functools.partial(task, half - 1) for task in (key_grads, value_grads, query_grads)]
        done = 0
        for i, low in enumerate(chunks if half < halves else ()):
            while done < len(tasks) and done * len(chunks) <= i * len(tasks):
                tasks[done]()
                done += 1
            soften(half, low)
        for task in tasks[done:]:
            task()
        if half and half % 2 == 0:
            stores += finish(half // 2 - 1)
    for copy in stores:
        copy.wait()


def attention(prepared, kv_pieces):
    q_rows, g_rows, q_cols, g_cols, live, rk, rv = prepared
    rows, kv_width = rk.shape
    groups = kv_width // HEAD_DIM
    flat = q_rows.shape[0]
    wide = (rows, flat // rows * HEAD_DIM)
    pieces = len(kv_pieces)
    chips = pieces // CORES
    piece_rows = kv_pieces[0][0].shape[-2]
    joined = [len(piece) == 1 for piece in kv_pieces]
    flat_pieces = sum(kv_pieces, [])
    keys = pieces * piece_rows + rows
    block = flat // groups // 2
    return pl.pallas_call(
        functools.partial(attention_kernel, chips, piece_rows, joined),
        in_specs=[VMEM_SPEC] * (7 + len(flat_pieces)),
        out_specs=[HBM_SPEC] * 3 + [VMEM_SPEC] * (2 * chips),
        out_shape=[shape(*wide), shape(rows, kv_width), shape(rows, kv_width)]
        + [jax.ShapeDtypeStruct((2, piece_rows, kv_width), F32)] * chips
        + [shape(2, piece_rows, kv_width)] * chips,
        scratch_shapes=[
            pltpu.VMEM((groups, keys, HEAD_DIM), BF16),
            pltpu.VMEM((groups, keys, 2 * HEAD_DIM), BF16),
            pltpu.VMEM((2, block, keys), F32),
            pltpu.VMEM((2, block, keys), F32),
            pltpu.VMEM((2, block, keys), BF16),
            pltpu.VMEM((2, block, keys), BF16),
            pltpu.VMEM(wide, BF16),
            pltpu.VMEM((rows, kv_width), BF16),
            pltpu.VMEM((rows, kv_width), BF16),
            pltpu.SemaphoreType.DMA((groups, 3)),
        ],
        compiler_params=PARAMS,
        cost_estimate=pl.CostEstimate(
            flops=10 * flat * keys * HEAD_DIM, bytes_accessed=10 * flat * HEAD_DIM, transcendentals=flat * keys
        ),
    )(live, q_rows, g_rows, q_cols, g_cols, rk, rv, *flat_pieces)


def exchange(x, links):
    routes = [(a, b) for pair in links for a, b in (pair, pair[::-1])]
    pairs = [(CORES * a + core, CORES * b + core) for a, b in routes for core in range(CORES)]
    return lax.ppermute(x, "seq", pairs)


def chip_links(chips, step):
    return [(chip, chip ^ step) for chip in range(chips) if chip < chip ^ step]


def swap_core(x, chips):
    pairs = [(CORES * chip + core, CORES * chip + 1 - core) for chip in range(chips) for core in range(CORES)]
    return lax.ppermute(x, "seq", pairs)


def local(chips, queries, outputs, out_grads, resp_keys, resp_values, lengths, prompt_keys, prompt_values):
    steps = list(range(1, chips))
    raw = [prompt_keys, prompt_values]
    kind = lax.broadcasted_iota(jnp.int32, (2,) + prompt_keys.shape, 0)
    kv = [jnp.where(kind == 0, prompt_keys[None], prompt_values[None])]
    far = [[exchange(x, chip_links(chips, step)) for x in (raw if step == 2 else kv)] for step in steps]
    prepared = prepare(lengths, queries[0], outputs[0], out_grads[0], resp_keys[0], resp_values[0])
    live = prepared[4]
    far = [[lax.optimization_barrier((x, live))[0] for x in piece] for piece in far]
    own = [kv] + far
    other = [[swap_core(x, chips) for x in piece] for piece in own]
    dq, drk, drv, *grads = attention(prepared, own + other)
    both = [grads[i] + swap_core(grads[chips + i], chips).astype(F32) for i in range(chips)]
    back = [exchange(both[step].astype(BF16), chip_links(chips, step)) for step in steps[1:] + steps[:1]]
    total = sum([x.astype(F32) for x in back], both[0]).astype(BF16)
    return dq[None], drk[None], drv[None], total[0], total[1]


def solution(mesh):
    chips = mesh.shape["seq"] // CORES
    split = ("dp", "seq")
    row3 = P(split, None, None)
    row2 = P(split, None)
    return jax.shard_map(
        functools.partial(local, chips),
        mesh=mesh,
        in_specs=(row3, row3, row3, row3, row3, P("dp"), row2, row2),
        out_specs=(row3, row3, row3, row2, row2),
        check_vma=False,
    )
```

```python
import functools

import jax
import jax.numpy as jnp
from jax import lax
from jax.experimental import pallas as pl
from jax.experimental.pallas import tpu as pltpu
from jax.sharding import PartitionSpec as P

HEAD_DIM = 128
SCALE = HEAD_DIM ** (-0.5)
LOG2E = 1.4426950408889634
NT = (((1,), (1,)), ((), ()))
CORES = 2
CHUNK = 32
DELTA_TERMS = 2
BF16 = jnp.bfloat16
F32 = jnp.float32
VMEM_SPEC = pl.BlockSpec(memory_space=pltpu.VMEM)
HBM_SPEC = pl.BlockSpec(memory_space=pltpu.HBM)
SMEM_SPEC = pl.BlockSpec(memory_space=pltpu.SMEM)
MIB = 1024 * 1024
PARAMS = pltpu.CompilerParams(vmem_limit_bytes=24 * MIB)


def shape(*dims):
    return jax.ShapeDtypeStruct(dims, BF16)


def dot(a, b, dims=None):
    if dims is None:
        return jnp.dot(a, b, preferred_element_type=F32)
    return lax.dot_general(a, b, dims, preferred_element_type=F32)


def head_slice(index):
    return slice(index * HEAD_DIM, (index + 1) * HEAD_DIM)


def in_hbm(*arrays):
    return [pltpu.with_memory_space_constraint(x, pltpu.HBM) for x in arrays]


def prepare_kernel(groups, len_ref, *refs):
    wide_in, narrow_in, refs = refs[:3], refs[3:5], refs[5:]
    (q_rows, g_rows, q_cols, g_cols, live_ref), narrow_out, refs = refs[:5], refs[5:7], refs[7:]
    wide_buf, (wide_sem, narrow_sem) = refs[:3], refs[3:]
    rows = wide_buf[0].shape[0]
    width = wide_buf[0].shape[1] // groups
    wide = [
        [
            pltpu.make_async_copy(src.at[:, group * width : (group + 1) * width], buf.at[:, group * width : (group + 1) * width], wide_sem.at[group, i])
            for i, (src, buf) in enumerate(zip(wide_in, wide_buf))
        ]
        for group in range(groups)
    ]
    narrow = [pltpu.make_async_copy(src, out, narrow_sem.at[i]) for i, (src, out) in enumerate(zip(narrow_in, narrow_out))]
    for copy in sum(wide, []) + narrow:
        copy.start()
    length = len_ref[lax.axis_index("seq")]
    live_ref[...] = jnp.where(lax.broadcasted_iota(jnp.int32, live_ref.shape, 0) < length, 1.0, 0.0)
    lane = lax.broadcasted_iota(jnp.int32, (rows, HEAD_DIM), 1)
    square = (HEAD_DIM, HEAD_DIM)
    same = lax.broadcasted_iota(jnp.int32, square, 0) == lax.broadcasted_iota(jnp.int32, square, 1)
    identity = jnp.where(same, 1.0, 0.0).astype(BF16)
    ones = jnp.ones((2 * HEAD_DIM, HEAD_DIM), BF16)
    q_ref, o_ref, g_ref = wide_buf
    heads = width // HEAD_DIM
    for group in range(groups):
        for copy in wide[group]:
            copy.wait()
        for head in range(group * heads, (group + 1) * heads):
            cols = head_slice(head)
            span = slice(head * rows, (head + 1) * rows)
            g = g_ref[:, cols]
            product = g.astype(F32) * o_ref[:, cols].astype(F32)
            high = product.astype(BF16)
            low = (product - high.astype(F32)).astype(BF16)
            left = dot(jnp.concatenate([high, low], axis=1), ones)
            terms = jnp.zeros((rows, HEAD_DIM), F32)
            for term in range(DELTA_TERMS):
                rounded = left.astype(BF16).astype(F32)
                terms = jnp.where(lane == term, rounded, terms)
                left = left - rounded
            q_rows[span, :] = q_ref[:, cols]
            g_rows[span, :HEAD_DIM] = g
            g_rows[span, HEAD_DIM:] = terms.astype(BF16)
        span = slice(group * heads * rows, (group + 1) * heads * rows)
        q_cols[:, span] = dot(identity, q_rows[span, :], NT).astype(BF16)
        g_cols[:, span] = dot(identity, g_rows[span, :HEAD_DIM], NT).astype(BF16)
    for copy in narrow:
        copy.wait()


def prepare(lengths, q, o, g, rk, rv):
    rows, width = q.shape
    groups = rk.shape[1] // HEAD_DIM
    flat = rows * width // HEAD_DIM
    narrow = [rk, rv]
    return pl.pallas_call(
        functools.partial(prepare_kernel, groups),
        in_specs=[SMEM_SPEC] + [HBM_SPEC] * 5,
        out_specs=[VMEM_SPEC] * 7,
        out_shape=[
            shape(flat, HEAD_DIM),
            shape(flat, 2 * HEAD_DIM),
            shape(HEAD_DIM, flat),
            shape(HEAD_DIM, flat),
            jax.ShapeDtypeStruct((rows, HEAD_DIM), F32),
        ]
        + [shape(*x.shape) for x in narrow],
        scratch_shapes=[pltpu.VMEM((rows, width), BF16)] * 3
        + [pltpu.SemaphoreType.DMA((groups, 3)), pltpu.SemaphoreType.DMA((2,))],
        compiler_params=PARAMS,
        cost_estimate=pl.CostEstimate(flops=rows * width * 4000, bytes_accessed=16 * rows * width, transcendentals=0),
    )(lengths, *in_hbm(q, o, g, *narrow))


def read_pieces(joined, refs):
    k_refs, v_refs = [], []
    for both in joined:
        k_refs.append(refs[0].at[0] if both else refs[0])
        v_refs.append(refs[0].at[1] if both else refs[1])
        refs = refs[1 if both else 2 :]
    return k_refs, v_refs, refs


def attention_kernel(chips, piece_rows, joined, live_ref, q_rows, g_rows, q_cols, g_cols, rk_ref, rv_ref, *rest):
    pieces = CORES * chips
    k_refs, v_refs, rest = read_pieces(joined, rest)
    (ds_ref, drk_ref, drv_ref), rest = rest[:3], rest[3:]
    d_own, d_other, rest = rest[:chips], rest[chips : 2 * chips], rest[2 * chips :]
    k_buf, v_buf, s_buf, dp_buf, p_buf = rest
    rows, width = rk_ref.shape
    groups = width // HEAD_DIM
    block = q_rows.shape[0] // groups // 2
    keys = k_buf.shape[1]
    prompt = keys - rows
    diagonal = lax.broadcasted_iota(jnp.int32, (CHUNK, rows), 1) - lax.broadcasted_iota(jnp.int32, (CHUNK, rows), 0)
    minus = jnp.where(lax.broadcasted_iota(jnp.int32, (keys, HEAD_DIM), 1) < DELTA_TERMS, -1.0, 0.0).astype(BF16)

    def place(half):
        return slice(half * block, (half + 1) * block)

    def load_keys(group):
        cols = head_slice(group)
        for i in range(pieces):
            span = slice(i * piece_rows, (i + 1) * piece_rows)
            k_buf[group, span, :] = k_refs[i][:, cols]
            v_buf[group, span, :HEAD_DIM] = v_refs[i][:, cols]
        k_buf[group, prompt:, :] = rk_ref[:, cols]
        v_buf[group, prompt:, :HEAD_DIM] = rv_ref[:, cols]
        v_buf[group, :, HEAD_DIM:] = minus

    def scores(half):
        s_buf[half % 2] = dot(q_rows[place(half), :], k_buf[half // 2], NT)

    def prob_grads(half):
        dp_buf[half % 2] = dot(g_rows[place(half), :], v_buf[half // 2], NT)

    def soften(half, low):
        slot = half % 2
        first = low % rows
        span = slice(low, low + CHUNK)
        s = s_buf[slot, span, :]
        s = jnp.concatenate([s[:, :prompt], jnp.where(diagonal > first, -1e30, s[:, prompt:])], axis=1)
        e = jnp.exp2((s - jnp.max(s, axis=1, keepdims=True)) * (SCALE * LOG2E))
        weight = (1.0 / jnp.sum(e, axis=1, keepdims=True)) * live_ref[first : first + CHUNK, :]
        p = e * jnp.concatenate([weight] * (keys // HEAD_DIM), axis=1)
        p_buf[slot, span, :] = p.astype(BF16)
        ds_ref[half * block + low : half * block + low + CHUNK, :] = (p * dp_buf[slot, span, :]).astype(BF16)

    halves = 2 * groups
    held = None
    for half in range(-1, halves):
        if half + 1 < halves:
            if (half + 1) % 2 == 0:
                load_keys((half + 1) // 2)
            scores(half + 1)
            prob_grads(half + 1)
        if half < 0:
            continue
        for low in range(0, block, CHUNK):
            soften(half, low)
        dk = dot(q_cols[:, place(half)], ds_ref[place(half), :])
        dv = dot(g_cols[:, place(half)], p_buf[half % 2])
        if half % 2 == 0:
            held = (dk, dv)
            continue
        cols = head_slice(half // 2)
        dk = ((held[0] + dk) * SCALE).T
        dv = (held[1] + dv).T
        for kind, grad in enumerate((dk, dv)):
            for i in range(chips):
                d_own[i][kind, :, cols] = grad[i * piece_rows : (i + 1) * piece_rows]
                d_other[i][kind, :, cols] = grad[(chips + i) * piece_rows : (chips + i + 1) * piece_rows].astype(BF16)
        drk_ref[:, cols] = dk[prompt:].astype(BF16)
        drv_ref[:, cols] = dv[prompt:].astype(BF16)


def attention(prepared, kv_pieces):
    q_rows, g_rows, q_cols, g_cols, live, rk, rv = prepared
    rows, kv_width = rk.shape
    groups = kv_width // HEAD_DIM
    flat = q_rows.shape[0]
    pieces = len(kv_pieces)
    chips = pieces // CORES
    piece_rows = kv_pieces[0][0].shape[-2]
    joined = [len(piece) == 1 for piece in kv_pieces]
    flat_pieces = sum(kv_pieces, [])
    keys = pieces * piece_rows + rows
    block = flat // groups // 2
    return pl.pallas_call(
        functools.partial(attention_kernel, chips, piece_rows, joined),
        in_specs=[VMEM_SPEC] * (7 + len(flat_pieces)),
        out_specs=[VMEM_SPEC] * (3 + 2 * chips),
        out_shape=[shape(flat, keys), shape(rows, kv_width), shape(rows, kv_width)]
        + [jax.ShapeDtypeStruct((2, piece_rows, kv_width), F32)] * chips
        + [shape(2, piece_rows, kv_width)] * chips,
        scratch_shapes=[
            pltpu.VMEM((groups, keys, HEAD_DIM), BF16),
            pltpu.VMEM((groups, keys, 2 * HEAD_DIM), BF16),
            pltpu.VMEM((2, block, keys), F32),
            pltpu.VMEM((2, block, keys), F32),
            pltpu.VMEM((2, block, keys), BF16),
        ],
        compiler_params=PARAMS,
        cost_estimate=pl.CostEstimate(
            flops=10 * flat * keys * HEAD_DIM, bytes_accessed=10 * flat * HEAD_DIM, transcendentals=flat * keys
        ),
    )(live, q_rows, g_rows, q_cols, g_cols, rk, rv, *flat_pieces)


def query_grad_kernel(joined, ds_ref, rk_ref, drk_in, drv_in, *rest):
    k_refs, _, rest = read_pieces(joined, rest)
    (dq_out, drk_out, drv_out), (k_buf, dq_buf, wide_sem, narrow_sem) = rest[:3], rest[3:]
    rows, width = rk_ref.shape
    groups = width // HEAD_DIM
    flat = ds_ref.shape[0] // groups
    step = dq_buf.shape[1] // groups
    copies = [
        pltpu.make_async_copy(src, out, narrow_sem.at[i]) for i, (src, out) in enumerate(((drk_in, drk_out), (drv_in, drv_out)))
    ]
    for copy in copies:
        copy.start()
    for group in range(groups):
        low = 0
        for ref in k_refs + [rk_ref]:
            k_buf[group, low : low + ref.shape[0], :] = ref[:, head_slice(group)]
            low += ref.shape[0]
        dq = (dot(ds_ref[group * flat : (group + 1) * flat, :], k_buf[group]) * SCALE).astype(BF16)
        for i in range(flat // rows):
            dq_buf[:, head_slice(group * (flat // rows) + i)] = dq[i * rows : (i + 1) * rows]
        part = slice(group * step, (group + 1) * step)
        copies.append(pltpu.make_async_copy(dq_buf.at[:, part], dq_out.at[:, part], wide_sem.at[group]))
        copies[-1].start()
    for copy in copies:
        copy.wait()


def query_grads(ds, rk, drk, drv, kv_pieces):
    rows, kv_width = rk.shape
    flat, keys = ds.shape
    groups = kv_width // HEAD_DIM
    wide = (rows, flat // rows * HEAD_DIM)
    joined = [len(piece) == 1 for piece in kv_pieces]
    flat_pieces = sum(kv_pieces, [])
    return pl.pallas_call(
        functools.partial(query_grad_kernel, joined),
        in_specs=[VMEM_SPEC] * (4 + len(flat_pieces)),
        out_specs=[HBM_SPEC] * 3,
        out_shape=[shape(*wide), shape(rows, kv_width), shape(rows, kv_width)],
        scratch_shapes=[
            pltpu.VMEM((groups, keys, HEAD_DIM), BF16),
            pltpu.VMEM(wide, BF16),
            pltpu.SemaphoreType.DMA((groups,)),
            pltpu.SemaphoreType.DMA((2,)),
        ],
        compiler_params=PARAMS,
        cost_estimate=pl.CostEstimate(flops=4 * flat * keys * HEAD_DIM, bytes_accessed=4 * flat * keys, transcendentals=0),
    )(ds, rk, drk, drv, *flat_pieces)


def exchange(x, links):
    routes = [(a, b) for pair in links for a, b in (pair, pair[::-1])]
    pairs = [(CORES * a + core, CORES * b + core) for a, b in routes for core in range(CORES)]
    return lax.ppermute(x, "seq", pairs)


def chip_links(chips, step):
    return [(chip, chip ^ step) for chip in range(chips) if chip < chip ^ step]


def swap_core(x, chips):
    pairs = [(CORES * chip + core, CORES * chip + 1 - core) for chip in range(chips) for core in range(CORES)]
    return lax.ppermute(x, "seq", pairs)


def local(chips, queries, outputs, out_grads, resp_keys, resp_values, lengths, prompt_keys, prompt_values):
    steps = list(range(1, chips))
    raw = [prompt_keys, prompt_values]
    kind = lax.broadcasted_iota(jnp.int32, (2,) + prompt_keys.shape, 0)
    kv = [jnp.where(kind == 0, prompt_keys[None], prompt_values[None])]
    far = [[exchange(x, chip_links(chips, step)) for x in (raw if step == 2 else kv)] for step in steps]
    prepared = prepare(lengths, queries[0], outputs[0], out_grads[0], resp_keys[0], resp_values[0])
    live = prepared[4]
    far[1] = [lax.optimization_barrier((x, live))[0] for x in far[1]]
    first = [swap_core(x, chips) for x in far[1]]
    far = [piece if i == 1 else [lax.optimization_barrier((x, first))[0] for x in piece] for i, piece in enumerate(far)]
    own = [kv] + far
    other = [first if i == 2 else [swap_core(x, chips) for x in piece] for i, piece in enumerate(own)]
    ds, drk, drv, *grads = attention(prepared, own + other)
    both = [None] * chips
    for step in [0] + steps[1:] + steps[:1]:
        both[step] = grads[step] + swap_core(grads[chips + step], chips).astype(F32)
    sent = [x.astype(BF16) for x in both]
    back = [exchange(sent[step], chip_links(chips, step)) for step in steps[1:] + steps[:1]]
    ds = lax.optimization_barrier((ds, [sent[step] for step in steps[1:] + steps[:1]]))[0]
    dq, drk, drv = query_grads(ds, prepared[5], drk, drv, own + other)
    dq, back[0] = lax.optimization_barrier((dq, back[0]))
    total = sum([x.astype(F32) for x in back], both[0]).astype(BF16)
    return dq[None], drk[None], drv[None], total[0], total[1]


def solution(mesh):
    chips = mesh.shape["seq"] // CORES
    split = ("dp", "seq")
    row3 = P(split, None, None)
    row2 = P(split, None)
    return jax.shard_map(
        functools.partial(local, chips),
        mesh=mesh,
        in_specs=(row3, row3, row3, row3, row3, P("dp"), row2, row2),
        out_specs=(row3, row3, row3, row2, row2),
        check_vma=False,
    )
```

```python
import functools

import jax
import jax.numpy as jnp
from jax import lax
from jax.experimental import pallas as pl
from jax.experimental.pallas import tpu as pltpu
from jax.sharding import PartitionSpec as P

HEAD_DIM = 128
SCALE = HEAD_DIM ** (-0.5)
LOG2E = 1.4426950408889634
NT = (((1,), (1,)), ((), ()))
CORES = 2
CHUNK = 32
DELTA_TERMS = 2
BF16 = jnp.bfloat16
F32 = jnp.float32
VMEM_SPEC = pl.BlockSpec(memory_space=pltpu.VMEM)
HBM_SPEC = pl.BlockSpec(memory_space=pltpu.HBM)
SMEM_SPEC = pl.BlockSpec(memory_space=pltpu.SMEM)
MIB = 1024 * 1024
PARAMS = pltpu.CompilerParams(vmem_limit_bytes=24 * MIB)


def shape(*dims):
    return jax.ShapeDtypeStruct(dims, BF16)


def dot(a, b, dims=None):
    if dims is None:
        return jnp.dot(a, b, preferred_element_type=F32)
    return lax.dot_general(a, b, dims, preferred_element_type=F32)


def head_slice(index):
    return slice(index * HEAD_DIM, (index + 1) * HEAD_DIM)


def in_hbm(*arrays):
    return [pltpu.with_memory_space_constraint(x, pltpu.HBM) for x in arrays]


def prepare_kernel(groups, *refs):
    len_in, refs = refs[0], refs[1:]
    wide_in, narrow_in, refs = refs[:3], refs[3:5], refs[5:]
    (q_rows, g_rows, q_cols, g_cols, live_ref), narrow_out, refs = refs[:5], refs[5:7], refs[7:]
    wide_buf, (len_ref, wide_sem, narrow_sem) = refs[:3], refs[3:]
    rows = wide_buf[0].shape[0]
    width = wide_buf[0].shape[1] // groups
    wide = [
        [
            pltpu.make_async_copy(src.at[:, group * width : (group + 1) * width], buf.at[:, group * width : (group + 1) * width], wide_sem.at[group, i])
            for i, (src, buf) in enumerate(zip(wide_in, wide_buf))
        ]
        for group in range(groups)
    ]
    narrow = [pltpu.make_async_copy(src, out, narrow_sem.at[i]) for i, (src, out) in enumerate(zip(narrow_in, narrow_out))]
    narrow.append(pltpu.make_async_copy(len_in, len_ref, narrow_sem.at[len(narrow)]))
    for copy in narrow[-1:] + sum(wide, []) + narrow[:-1]:
        copy.start()
    lane = lax.broadcasted_iota(jnp.int32, (rows, HEAD_DIM), 1)
    square = (HEAD_DIM, HEAD_DIM)
    same = lax.broadcasted_iota(jnp.int32, square, 0) == lax.broadcasted_iota(jnp.int32, square, 1)
    identity = jnp.where(same, 1.0, 0.0).astype(BF16)
    ones = jnp.ones((2 * HEAD_DIM, HEAD_DIM), BF16)
    q_ref, o_ref, g_ref = wide_buf
    heads = width // HEAD_DIM
    for group in range(groups):
        for copy in wide[group]:
            copy.wait()
        for head in range(group * heads, (group + 1) * heads):
            cols = head_slice(head)
            span = slice(head * rows, (head + 1) * rows)
            g = g_ref[:, cols]
            product = g.astype(F32) * o_ref[:, cols].astype(F32)
            high = product.astype(BF16)
            low = (product - high.astype(F32)).astype(BF16)
            left = dot(jnp.concatenate([high, low], axis=1), ones)
            terms = jnp.zeros((rows, HEAD_DIM), F32)
            for term in range(DELTA_TERMS):
                rounded = left.astype(BF16).astype(F32)
                terms = jnp.where(lane == term, rounded, terms)
                left = left - rounded
            q_rows[span, :] = q_ref[:, cols]
            g_rows[span, :HEAD_DIM] = g
            g_rows[span, HEAD_DIM:] = terms.astype(BF16)
        span = slice(group * heads * rows, (group + 1) * heads * rows)
        q_cols[:, span] = dot(identity, q_rows[span, :], NT).astype(BF16)
        g_cols[:, span] = dot(identity, g_rows[span, :HEAD_DIM], NT).astype(BF16)
    for copy in narrow:
        copy.wait()
    length = len_ref[lax.axis_index("seq")]
    live_ref[...] = jnp.where(lax.broadcasted_iota(jnp.int32, live_ref.shape, 0) < length, 1.0, 0.0)


def prepare(lengths, q, o, g, rk, rv):
    rows, width = q.shape
    groups = rk.shape[1] // HEAD_DIM
    flat = rows * width // HEAD_DIM
    narrow = [rk, rv]
    return pl.pallas_call(
        functools.partial(prepare_kernel, groups),
        in_specs=[HBM_SPEC] * 6,
        out_specs=[VMEM_SPEC] * 7,
        out_shape=[
            shape(flat, HEAD_DIM),
            shape(flat, 2 * HEAD_DIM),
            shape(HEAD_DIM, flat),
            shape(HEAD_DIM, flat),
            jax.ShapeDtypeStruct((rows, HEAD_DIM), F32),
        ]
        + [shape(*x.shape) for x in narrow],
        scratch_shapes=[pltpu.VMEM((rows, width), BF16)] * 3
        + [pltpu.SMEM(lengths.shape, jnp.int32), pltpu.SemaphoreType.DMA((groups, 3)), pltpu.SemaphoreType.DMA((3,))],
        compiler_params=PARAMS,
        cost_estimate=pl.CostEstimate(flops=rows * width * 4000, bytes_accessed=16 * rows * width, transcendentals=0),
    )(*in_hbm(lengths, q, o, g, *narrow))


def read_pieces(joined, refs):
    k_refs, v_refs = [], []
    for both in joined:
        k_refs.append(refs[0].at[0] if both else refs[0])
        v_refs.append(refs[0].at[1] if both else refs[1])
        refs = refs[1 if both else 2 :]
    return k_refs, v_refs, refs


def attention_kernel(chips, piece_rows, joined, live_ref, q_rows, g_rows, q_cols, g_cols, rk_ref, rv_ref, *rest):
    pieces = CORES * chips
    k_refs, v_refs, rest = read_pieces(joined, rest)
    (ds_ref, drk_ref, drv_ref), rest = rest[:3], rest[3:]
    d_own, d_other, rest = rest[:chips], rest[chips : 2 * chips], rest[2 * chips :]
    k_buf, v_buf, s_buf, dp_buf, p_buf = rest
    rows, width = rk_ref.shape
    groups = width // HEAD_DIM
    block = q_rows.shape[0] // groups // 2
    keys = k_buf.shape[1]
    prompt = keys - rows
    diagonal = lax.broadcasted_iota(jnp.int32, (CHUNK, rows), 1) - lax.broadcasted_iota(jnp.int32, (CHUNK, rows), 0)
    minus = jnp.where(lax.broadcasted_iota(jnp.int32, (keys, HEAD_DIM), 1) < DELTA_TERMS, -1.0, 0.0).astype(BF16)

    def place(half):
        return slice(half * block, (half + 1) * block)

    def load_keys(group):
        cols = head_slice(group)
        for i in range(pieces):
            span = slice(i * piece_rows, (i + 1) * piece_rows)
            k_buf[group, span, :] = k_refs[i][:, cols]
            v_buf[group, span, :HEAD_DIM] = v_refs[i][:, cols]
        k_buf[group, prompt:, :] = rk_ref[:, cols]
        v_buf[group, prompt:, :HEAD_DIM] = rv_ref[:, cols]
        v_buf[group, :, HEAD_DIM:] = minus

    def scores(half):
        s_buf[half % 2] = dot(q_rows[place(half), :], k_buf[half // 2], NT)

    def prob_grads(half):
        dp_buf[half % 2] = dot(g_rows[place(half), :], v_buf[half // 2], NT)

    def soften(half, low):
        slot = half % 2
        first = low % rows
        span = slice(low, low + CHUNK)
        s = s_buf[slot, span, :]
        s = jnp.concatenate([s[:, :prompt], jnp.where(diagonal > first, -1e30, s[:, prompt:])], axis=1)
        e = jnp.exp2((s - jnp.max(s, axis=1, keepdims=True)) * (SCALE * LOG2E))
        weight = (1.0 / jnp.sum(e, axis=1, keepdims=True)) * live_ref[first : first + CHUNK, :]
        p = e * jnp.concatenate([weight] * (keys // HEAD_DIM), axis=1)
        p_buf[slot, span, :] = p.astype(BF16)
        ds_ref[half * block + low : half * block + low + CHUNK, :] = (p * dp_buf[slot, span, :]).astype(BF16)

    halves = 2 * groups
    held = None
    for half in range(-1, halves):
        if half + 1 < halves:
            if (half + 1) % 2 == 0:
                load_keys((half + 1) // 2)
            scores(half + 1)
            prob_grads(half + 1)
        if half < 0:
            continue
        for low in range(0, block, CHUNK):
            soften(half, low)
        dk = dot(q_cols[:, place(half)], ds_ref[place(half), :])
        dv = dot(g_cols[:, place(half)], p_buf[half % 2])
        if half % 2 == 0:
            held = (dk, dv)
            continue
        cols = head_slice(half // 2)
        dk = ((held[0] + dk) * SCALE).T
        dv = (held[1] + dv).T
        for kind, grad in enumerate((dk, dv)):
            for i in range(chips):
                d_own[i][kind, :, cols] = grad[i * piece_rows : (i + 1) * piece_rows]
                d_other[i][kind, :, cols] = grad[(chips + i) * piece_rows : (chips + i + 1) * piece_rows].astype(BF16)
        drk_ref[:, cols] = dk[prompt:].astype(BF16)
        drv_ref[:, cols] = dv[prompt:].astype(BF16)


def attention(prepared, kv_pieces):
    q_rows, g_rows, q_cols, g_cols, live, rk, rv = prepared
    rows, kv_width = rk.shape
    groups = kv_width // HEAD_DIM
    flat = q_rows.shape[0]
    pieces = len(kv_pieces)
    chips = pieces // CORES
    piece_rows = kv_pieces[0][0].shape[-2]
    joined = [len(piece) == 1 for piece in kv_pieces]
    flat_pieces = sum(kv_pieces, [])
    keys = pieces * piece_rows + rows
    block = flat // groups // 2
    return pl.pallas_call(
        functools.partial(attention_kernel, chips, piece_rows, joined),
        in_specs=[VMEM_SPEC] * (7 + len(flat_pieces)),
        out_specs=[VMEM_SPEC] * (3 + 2 * chips),
        out_shape=[shape(flat, keys), shape(rows, kv_width), shape(rows, kv_width)]
        + [jax.ShapeDtypeStruct((2, piece_rows, kv_width), F32)] * chips
        + [shape(2, piece_rows, kv_width)] * chips,
        scratch_shapes=[
            pltpu.VMEM((groups, keys, HEAD_DIM), BF16),
            pltpu.VMEM((groups, keys, 2 * HEAD_DIM), BF16),
            pltpu.VMEM((2, block, keys), F32),
            pltpu.VMEM((2, block, keys), F32),
            pltpu.VMEM((2, block, keys), BF16),
        ],
        compiler_params=PARAMS,
        cost_estimate=pl.CostEstimate(
            flops=10 * flat * keys * HEAD_DIM, bytes_accessed=10 * flat * HEAD_DIM, transcendentals=flat * keys
        ),
    )(live, q_rows, g_rows, q_cols, g_cols, rk, rv, *flat_pieces)


def query_grad_kernel(joined, ds_ref, rk_ref, drk_in, drv_in, *rest):
    k_refs, _, rest = read_pieces(joined, rest)
    (dq_out, drk_out, drv_out), (k_buf, dq_buf, wide_sem, narrow_sem) = rest[:3], rest[3:]
    rows, width = rk_ref.shape
    groups = width // HEAD_DIM
    flat = ds_ref.shape[0] // groups
    step = dq_buf.shape[1] // groups
    copies = [
        pltpu.make_async_copy(src, out, narrow_sem.at[i]) for i, (src, out) in enumerate(((drk_in, drk_out), (drv_in, drv_out)))
    ]
    for copy in copies:
        copy.start()
    for group in range(groups):
        low = 0
        for ref in k_refs + [rk_ref]:
            k_buf[group, low : low + ref.shape[0], :] = ref[:, head_slice(group)]
            low += ref.shape[0]
        dq = (dot(ds_ref[group * flat : (group + 1) * flat, :], k_buf[group]) * SCALE).astype(BF16)
        for i in range(flat // rows):
            dq_buf[:, head_slice(group * (flat // rows) + i)] = dq[i * rows : (i + 1) * rows]
        part = slice(group * step, (group + 1) * step)
        copies.append(pltpu.make_async_copy(dq_buf.at[:, part], dq_out.at[:, part], wide_sem.at[group]))
        copies[-1].start()
    for copy in copies:
        copy.wait()


def query_grads(ds, rk, drk, drv, kv_pieces):
    rows, kv_width = rk.shape
    flat, keys = ds.shape
    groups = kv_width // HEAD_DIM
    wide = (rows, flat // rows * HEAD_DIM)
    joined = [len(piece) == 1 for piece in kv_pieces]
    flat_pieces = sum(kv_pieces, [])
    return pl.pallas_call(
        functools.partial(query_grad_kernel, joined),
        in_specs=[VMEM_SPEC] * (4 + len(flat_pieces)),
        out_specs=[HBM_SPEC] * 3,
        out_shape=[shape(*wide), shape(rows, kv_width), shape(rows, kv_width)],
        scratch_shapes=[
            pltpu.VMEM((groups, keys, HEAD_DIM), BF16),
            pltpu.VMEM(wide, BF16),
            pltpu.SemaphoreType.DMA((groups,)),
            pltpu.SemaphoreType.DMA((2,)),
        ],
        compiler_params=PARAMS,
        cost_estimate=pl.CostEstimate(flops=4 * flat * keys * HEAD_DIM, bytes_accessed=4 * flat * keys, transcendentals=0),
    )(ds, rk, drk, drv, *flat_pieces)


def exchange(x, links):
    routes = [(a, b) for pair in links for a, b in (pair, pair[::-1])]
    pairs = [(CORES * a + core, CORES * b + core) for a, b in routes for core in range(CORES)]
    return lax.ppermute(x, "seq", pairs)


def chip_links(chips, step):
    return [(chip, chip ^ step) for chip in range(chips) if chip < chip ^ step]


def swap_core(x, chips):
    pairs = [(CORES * chip + core, CORES * chip + 1 - core) for chip in range(chips) for core in range(CORES)]
    return lax.ppermute(x, "seq", pairs)


def local(chips, queries, outputs, out_grads, resp_keys, resp_values, lengths, prompt_keys, prompt_values):
    steps = list(range(1, chips))
    raw = [prompt_keys, prompt_values]
    kind = lax.broadcasted_iota(jnp.int32, (2,) + prompt_keys.shape, 0)
    kv = [jnp.where(kind == 0, prompt_keys[None], prompt_values[None])]
    far = [[exchange(x, chip_links(chips, step)) for x in (raw if step == 2 else kv)] for step in steps]
    prepared = prepare(lengths, queries[0], outputs[0], out_grads[0], resp_keys[0], resp_values[0])
    live = prepared[4]
    far[1] = [lax.optimization_barrier((x, live))[0] for x in far[1]]
    first = [swap_core(x, chips) for x in far[1]]
    far = [piece if i == 1 else [lax.optimization_barrier((x, first))[0] for x in piece] for i, piece in enumerate(far)]
    own = [kv] + far
    other = [first if i == 2 else [swap_core(x, chips) for x in piece] for i, piece in enumerate(own)]
    ds, drk, drv, *grads = attention(prepared, own + other)
    both = [None] * chips
    for step in [0] + steps[1:] + steps[:1]:
        both[step] = grads[step] + swap_core(grads[chips + step], chips).astype(F32)
    sent = [x.astype(BF16) for x in both]
    back = [exchange(sent[step], chip_links(chips, step)) for step in steps[1:] + steps[:1]]
    ds = lax.optimization_barrier((ds, [sent[step] for step in steps[1:] + steps[:1]]))[0]
    dq, drk, drv = query_grads(ds, prepared[5], drk, drv, own + other)
    dq, back[0] = lax.optimization_barrier((dq, back[0]))
    total = sum([x.astype(F32) for x in back], both[0]).astype(BF16)
    return dq[None], drk[None], drv[None], total[0], total[1]


def solution(mesh):
    chips = mesh.shape["seq"] // CORES
    split = ("dp", "seq")
    row3 = P(split, None, None)
    row2 = P(split, None)
    return jax.shard_map(
        functools.partial(local, chips),
        mesh=mesh,
        in_specs=(row3, row3, row3, row3, row3, P("dp"), row2, row2),
        out_specs=(row3, row3, row3, row2, row2),
        check_vma=False,
    )
```

```python
import functools

import jax
import jax.numpy as jnp
from jax import lax
from jax.experimental import pallas as pl
from jax.experimental.pallas import tpu as pltpu
from jax.sharding import PartitionSpec as P

HEAD_DIM = 128
SCALE = HEAD_DIM ** (-0.5)
LOG2E = 1.4426950408889634
NT = (((1,), (1,)), ((), ()))
CORES = 2
CHUNK = 32
DELTA_TERMS = 2
BF16 = jnp.bfloat16
F32 = jnp.float32
VMEM_SPEC = pl.BlockSpec(memory_space=pltpu.VMEM)
HBM_SPEC = pl.BlockSpec(memory_space=pltpu.HBM)
SMEM_SPEC = pl.BlockSpec(memory_space=pltpu.SMEM)
MIB = 1024 * 1024
PARAMS = pltpu.CompilerParams(vmem_limit_bytes=24 * MIB)


def shape(*dims):
    return jax.ShapeDtypeStruct(dims, BF16)


def dot(a, b, dims=None):
    if dims is None:
        return jnp.dot(a, b, preferred_element_type=F32)
    return lax.dot_general(a, b, dims, preferred_element_type=F32)


def head_slice(index):
    return slice(index * HEAD_DIM, (index + 1) * HEAD_DIM)


def in_hbm(*arrays):
    return [pltpu.with_memory_space_constraint(x, pltpu.HBM) for x in arrays]


def prepare_kernel(groups, *refs):
    len_in, refs = refs[0], refs[1:]
    wide_in, narrow_in, refs = refs[:3], refs[3:5], refs[5:]
    (q_rows, g_rows, q_cols, g_cols, live_ref), narrow_out, refs = refs[:5], refs[5:7], refs[7:]
    wide_buf, (len_ref, wide_sem, narrow_sem) = refs[:3], refs[3:]
    rows = wide_buf[0].shape[0]
    width = wide_buf[0].shape[1] // groups
    wide = [
        [
            pltpu.make_async_copy(src.at[:, group * width : (group + 1) * width], buf.at[:, group * width : (group + 1) * width], wide_sem.at[group, i])
            for i, (src, buf) in enumerate(zip(wide_in, wide_buf))
        ]
        for group in range(groups)
    ]
    narrow = [pltpu.make_async_copy(src, out, narrow_sem.at[i]) for i, (src, out) in enumerate(zip(narrow_in, narrow_out))]
    narrow.append(pltpu.make_async_copy(len_in, len_ref, narrow_sem.at[len(narrow)]))
    for copy in narrow[-1:] + sum(wide, []) + narrow[:-1]:
        copy.start()
    lane = lax.broadcasted_iota(jnp.int32, (rows, HEAD_DIM), 1)
    square = (HEAD_DIM, HEAD_DIM)
    same = lax.broadcasted_iota(jnp.int32, square, 0) == lax.broadcasted_iota(jnp.int32, square, 1)
    identity = jnp.where(same, 1.0, 0.0).astype(BF16)
    ones = jnp.ones((2 * HEAD_DIM, HEAD_DIM), BF16)
    q_ref, o_ref, g_ref = wide_buf
    heads = width // HEAD_DIM
    for group in range(groups):
        for copy in wide[group]:
            copy.wait()
        for head in range(group * heads, (group + 1) * heads):
            cols = head_slice(head)
            span = slice(head * rows, (head + 1) * rows)
            g = g_ref[:, cols]
            product = g.astype(F32) * o_ref[:, cols].astype(F32)
            high = product.astype(BF16)
            low = (product - high.astype(F32)).astype(BF16)
            left = dot(jnp.concatenate([high, low], axis=1), ones)
            terms = jnp.zeros((rows, HEAD_DIM), F32)
            for term in range(DELTA_TERMS):
                rounded = left.astype(BF16).astype(F32)
                terms = jnp.where(lane == term, rounded, terms)
                left = left - rounded
            q_rows[span, :] = q_ref[:, cols]
            g_rows[span, :HEAD_DIM] = g
            g_rows[span, HEAD_DIM:] = terms.astype(BF16)
        span = slice(group * heads * rows, (group + 1) * heads * rows)
        q_cols[:, span] = dot(identity, q_rows[span, :], NT).astype(BF16)
        g_cols[:, span] = dot(identity, g_rows[span, :HEAD_DIM], NT).astype(BF16)
    for copy in narrow:
        copy.wait()
    length = len_ref[lax.axis_index("seq")]
    live_ref[...] = jnp.where(lax.broadcasted_iota(jnp.int32, live_ref.shape, 0) < length, 1.0, 0.0)


def prepare(lengths, q, o, g, rk, rv):
    rows, width = q.shape
    groups = rk.shape[1] // HEAD_DIM
    flat = rows * width // HEAD_DIM
    narrow = [rk, rv]
    return pl.pallas_call(
        functools.partial(prepare_kernel, groups),
        in_specs=[HBM_SPEC] * 6,
        out_specs=[VMEM_SPEC] * 7,
        out_shape=[
            shape(flat, HEAD_DIM),
            shape(flat, 2 * HEAD_DIM),
            shape(HEAD_DIM, flat),
            shape(HEAD_DIM, flat),
            jax.ShapeDtypeStruct((rows, HEAD_DIM), F32),
        ]
        + [shape(*x.shape) for x in narrow],
        scratch_shapes=[pltpu.VMEM((rows, width), BF16)] * 3
        + [pltpu.SMEM(lengths.shape, jnp.int32), pltpu.SemaphoreType.DMA((groups, 3)), pltpu.SemaphoreType.DMA((3,))],
        compiler_params=PARAMS,
        cost_estimate=pl.CostEstimate(flops=rows * width * 4000, bytes_accessed=16 * rows * width, transcendentals=0),
    )(*in_hbm(lengths, q, o, g, *narrow))


def read_pieces(joined, refs):
    k_refs, v_refs = [], []
    for both in joined:
        k_refs.append(refs[0].at[0] if both else refs[0])
        v_refs.append(refs[0].at[1] if both else refs[1])
        refs = refs[1 if both else 2 :]
    return k_refs, v_refs, refs


def attention_kernel(chips, piece_rows, joined, live_ref, q_rows, g_rows, q_cols, g_cols, rk_ref, rv_ref, *rest):
    pieces = CORES * chips
    k_refs, v_refs, rest = read_pieces(joined, rest)
    (ds_ref, drk_ref, drv_ref), rest = rest[:3], rest[3:]
    d_own, d_other, rest = rest[:chips], rest[chips : 2 * chips], rest[2 * chips :]
    k_buf, v_buf, s_buf, dp_buf, p_buf = rest
    rows, width = rk_ref.shape
    groups = width // HEAD_DIM
    block = q_rows.shape[0] // groups // 2
    keys = k_buf.shape[1]
    prompt = keys - rows
    diagonal = lax.broadcasted_iota(jnp.int32, (CHUNK, rows), 1) - lax.broadcasted_iota(jnp.int32, (CHUNK, rows), 0)
    minus = jnp.where(lax.broadcasted_iota(jnp.int32, (keys, HEAD_DIM), 1) < DELTA_TERMS, -1.0, 0.0).astype(BF16)

    def place(half):
        return slice(half * block, (half + 1) * block)

    def load_keys(group):
        cols = head_slice(group)
        for i in range(pieces):
            span = slice(i * piece_rows, (i + 1) * piece_rows)
            k_buf[group, span, :] = k_refs[i][:, cols]
            v_buf[group, span, :HEAD_DIM] = v_refs[i][:, cols]
        k_buf[group, prompt:, :] = rk_ref[:, cols]
        v_buf[group, prompt:, :HEAD_DIM] = rv_ref[:, cols]
        v_buf[group, :, HEAD_DIM:] = minus

    def scores(half):
        s_buf[half % 2] = dot(q_rows[place(half), :], k_buf[half // 2], NT)

    def prob_grads(half):
        dp_buf[half % 2] = dot(g_rows[place(half), :], v_buf[half // 2], NT)

    def soften(half, low):
        slot = half % 2
        first = low % rows
        span = slice(low, low + CHUNK)
        s = s_buf[slot, span, :]
        s = jnp.concatenate([s[:, :prompt], jnp.where(diagonal > first, -1e30, s[:, prompt:])], axis=1)
        e = jnp.exp2((s - jnp.max(s, axis=1, keepdims=True)) * (SCALE * LOG2E))
        weight = (1.0 / jnp.sum(e, axis=1, keepdims=True)) * live_ref[first : first + CHUNK, :]
        p = e * jnp.concatenate([weight] * (keys // HEAD_DIM), axis=1)
        p_buf[slot, span, :] = p.astype(BF16)
        ds_ref[half * block + low : half * block + low + CHUNK, :] = (p * dp_buf[slot, span, :]).astype(BF16)

    halves = 2 * groups
    held = None
    for half in range(-1, halves):
        if half + 1 < halves:
            if (half + 1) % 2 == 0:
                load_keys((half + 1) // 2)
            scores(half + 1)
            prob_grads(half + 1)
        if half < 0:
            continue
        for low in range(0, block, CHUNK):
            soften(half, low)
        dk = dot(q_cols[:, place(half)], ds_ref[place(half), :])
        dv = dot(g_cols[:, place(half)], p_buf[half % 2])
        if half % 2 == 0:
            held = (dk, dv)
            continue
        cols = head_slice(half // 2)
        dk = ((held[0] + dk) * SCALE).T
        dv = (held[1] + dv).T
        for kind, grad in enumerate((dk, dv)):
            for i in range(chips):
                d_own[i][kind, :, cols] = grad[i * piece_rows : (i + 1) * piece_rows]
                d_other[i][kind, :, cols] = grad[(chips + i) * piece_rows : (chips + i + 1) * piece_rows].astype(BF16)
        drk_ref[:, cols] = dk[prompt:].astype(BF16)
        drv_ref[:, cols] = dv[prompt:].astype(BF16)


def attention(prepared, kv_pieces):
    q_rows, g_rows, q_cols, g_cols, live, rk, rv = prepared
    rows, kv_width = rk.shape
    groups = kv_width // HEAD_DIM
    flat = q_rows.shape[0]
    pieces = len(kv_pieces)
    chips = pieces // CORES
    piece_rows = kv_pieces[0][0].shape[-2]
    joined = [len(piece) == 1 for piece in kv_pieces]
    flat_pieces = sum(kv_pieces, [])
    keys = pieces * piece_rows + rows
    block = flat // groups // 2
    return pl.pallas_call(
        functools.partial(attention_kernel, chips, piece_rows, joined),
        in_specs=[VMEM_SPEC] * (7 + len(flat_pieces)),
        out_specs=[VMEM_SPEC] * (3 + 2 * chips),
        out_shape=[shape(flat, keys), shape(rows, kv_width), shape(rows, kv_width)]
        + [jax.ShapeDtypeStruct((2, piece_rows, kv_width), F32)] * chips
        + [shape(2, piece_rows, kv_width)] * chips,
        scratch_shapes=[
            pltpu.VMEM((groups, keys, HEAD_DIM), BF16),
            pltpu.VMEM((groups, keys, 2 * HEAD_DIM), BF16),
            pltpu.VMEM((2, block, keys), F32),
            pltpu.VMEM((2, block, keys), F32),
            pltpu.VMEM((2, block, keys), BF16),
        ],
        compiler_params=PARAMS,
        cost_estimate=pl.CostEstimate(
            flops=10 * flat * keys * HEAD_DIM, bytes_accessed=10 * flat * HEAD_DIM, transcendentals=flat * keys
        ),
    )(live, q_rows, g_rows, q_cols, g_cols, rk, rv, *flat_pieces)


def query_grad_kernel(joined, ds_ref, rk_ref, drk_in, drv_in, *rest):
    k_refs, _, rest = read_pieces(joined, rest)
    (dq_out, drk_out, drv_out), (k_buf, dq_buf, wide_sem, narrow_sem) = rest[:3], rest[3:]
    rows, width = rk_ref.shape
    groups = width // HEAD_DIM
    flat = ds_ref.shape[0] // groups
    step = dq_buf.shape[1] // groups
    copies = [
        pltpu.make_async_copy(src, out, narrow_sem.at[i]) for i, (src, out) in enumerate(((drk_in, drk_out), (drv_in, drv_out)))
    ]
    for copy in copies:
        copy.start()
    for group in range(groups):
        low = 0
        for ref in k_refs + [rk_ref]:
            k_buf[group, low : low + ref.shape[0], :] = ref[:, head_slice(group)]
            low += ref.shape[0]
        dq = (dot(ds_ref[group * flat : (group + 1) * flat, :], k_buf[group]) * SCALE).astype(BF16)
        for i in range(flat // rows):
            dq_buf[:, head_slice(group * (flat // rows) + i)] = dq[i * rows : (i + 1) * rows]
        part = slice(group * step, (group + 1) * step)
        copies.append(pltpu.make_async_copy(dq_buf.at[:, part], dq_out.at[:, part], wide_sem.at[group]))
        copies[-1].start()
    for copy in copies:
        copy.wait()


def query_grads(ds, rk, drk, drv, kv_pieces):
    rows, kv_width = rk.shape
    flat, keys = ds.shape
    groups = kv_width // HEAD_DIM
    wide = (rows, flat // rows * HEAD_DIM)
    joined = [len(piece) == 1 for piece in kv_pieces]
    flat_pieces = sum(kv_pieces, [])
    return pl.pallas_call(
        functools.partial(query_grad_kernel, joined),
        in_specs=[VMEM_SPEC] * (4 + len(flat_pieces)),
        out_specs=[HBM_SPEC] * 3,
        out_shape=[shape(*wide), shape(rows, kv_width), shape(rows, kv_width)],
        scratch_shapes=[
            pltpu.VMEM((groups, keys, HEAD_DIM), BF16),
            pltpu.VMEM(wide, BF16),
            pltpu.SemaphoreType.DMA((groups,)),
            pltpu.SemaphoreType.DMA((2,)),
        ],
        compiler_params=PARAMS,
        cost_estimate=pl.CostEstimate(flops=4 * flat * keys * HEAD_DIM, bytes_accessed=4 * flat * keys, transcendentals=0),
    )(ds, rk, drk, drv, *flat_pieces)


def exchange(x, links):
    routes = [(a, b) for pair in links for a, b in (pair, pair[::-1])]
    pairs = [(CORES * a + core, CORES * b + core) for a, b in routes for core in range(CORES)]
    return lax.ppermute(x, "seq", pairs)


def chip_links(chips, step):
    return [(chip, chip ^ step) for chip in range(chips) if chip < chip ^ step]


def swap_core(x, chips):
    pairs = [(CORES * chip + core, CORES * chip + 1 - core) for chip in range(chips) for core in range(CORES)]
    return lax.ppermute(x, "seq", pairs)


def local(chips, queries, outputs, out_grads, resp_keys, resp_values, lengths, prompt_keys, prompt_values):
    steps = list(range(1, chips))
    raw = [prompt_keys, prompt_values]
    kind = lax.broadcasted_iota(jnp.int32, (2,) + prompt_keys.shape, 0)
    kv = [jnp.where(kind == 0, prompt_keys[None], prompt_values[None])]
    far = [[exchange(x, chip_links(chips, step)) for x in (raw if step == 2 else kv)] for step in steps]
    prepared = prepare(lengths, queries[0], outputs[0], out_grads[0], resp_keys[0], resp_values[0])
    live = prepared[4]
    far[1] = [lax.optimization_barrier((x, live))[0] for x in far[1]]
    first = [swap_core(x, chips) for x in far[1]]
    far = [piece if i == 1 else [lax.optimization_barrier((x, first))[0] for x in piece] for i, piece in enumerate(far)]
    own = [kv] + far
    other = [first if i == 2 else [swap_core(x, chips) for x in piece] for i, piece in enumerate(own)]
    ds, drk, drv, *grads = attention(prepared, own + other)
    both = [None] * chips
    for step in steps[1:] + steps[:1]:
        both[step] = grads[step] + swap_core(grads[chips + step], chips).astype(F32)
    sent = [x.astype(BF16) for x in both[1:]]
    home = lax.optimization_barrier((grads[chips], sent[0]))[0]
    both[0] = grads[0] + swap_core(home, chips).astype(F32)
    back = [exchange(sent[step - 1], chip_links(chips, step)) for step in steps[1:] + steps[:1]]
    ds = lax.optimization_barrier((ds, [sent[step - 1] for step in steps[1:] + steps[:1]]))[0]
    dq, drk, drv = query_grads(ds, prepared[5], drk, drv, own + other)
    dq, back[0] = lax.optimization_barrier((dq, back[0]))
    total = sum([x.astype(F32) for x in back], both[0]).astype(BF16)
    return dq[None], drk[None], drv[None], total[0], total[1]


def solution(mesh):
    chips = mesh.shape["seq"] // CORES
    split = ("dp", "seq")
    row3 = P(split, None, None)
    row2 = P(split, None)
    return jax.shard_map(
        functools.partial(local, chips),
        mesh=mesh,
        in_specs=(row3, row3, row3, row3, row3, P("dp"), row2, row2),
        out_specs=(row3, row3, row3, row2, row2),
        check_vma=False,
    )
```

```python
import functools

import jax
import jax.numpy as jnp
from jax import lax
from jax.experimental import pallas as pl
from jax.experimental.pallas import tpu as pltpu
from jax.sharding import PartitionSpec as P

HEAD_DIM = 128
SCALE = HEAD_DIM ** (-0.5)
LOG2E = 1.4426950408889634
NT = (((1,), (1,)), ((), ()))
CORES = 2
CHUNK = 16
DELTA_TERMS = 2
BF16 = jnp.bfloat16
F32 = jnp.float32
VMEM_SPEC = pl.BlockSpec(memory_space=pltpu.VMEM)
HBM_SPEC = pl.BlockSpec(memory_space=pltpu.HBM)
SMEM_SPEC = pl.BlockSpec(memory_space=pltpu.SMEM)
MIB = 1024 * 1024
PARAMS = pltpu.CompilerParams(vmem_limit_bytes=24 * MIB)


def shape(*dims):
    return jax.ShapeDtypeStruct(dims, BF16)


def dot(a, b, dims=None):
    if dims is None:
        return jnp.dot(a, b, preferred_element_type=F32)
    return lax.dot_general(a, b, dims, preferred_element_type=F32)


def head_slice(index):
    return slice(index * HEAD_DIM, (index + 1) * HEAD_DIM)


def in_hbm(*arrays):
    return [pltpu.with_memory_space_constraint(x, pltpu.HBM) for x in arrays]


def prepare_kernel(groups, *refs):
    len_in, refs = refs[0], refs[1:]
    wide_in, narrow_in, refs = refs[:3], refs[3:5], refs[5:]
    (q_rows, g_rows, q_cols, g_cols, live_ref), narrow_out, refs = refs[:5], refs[5:7], refs[7:]
    wide_buf, (len_ref, wide_sem, narrow_sem) = refs[:3], refs[3:]
    rows = wide_buf[0].shape[0]
    width = wide_buf[0].shape[1] // groups
    wide = [
        [
            pltpu.make_async_copy(src.at[:, group * width : (group + 1) * width], buf.at[:, group * width : (group + 1) * width], wide_sem.at[group, i])
            for i, (src, buf) in enumerate(zip(wide_in, wide_buf))
        ]
        for group in range(groups)
    ]
    narrow = [pltpu.make_async_copy(src, out, narrow_sem.at[i]) for i, (src, out) in enumerate(zip(narrow_in, narrow_out))]
    narrow.append(pltpu.make_async_copy(len_in, len_ref, narrow_sem.at[len(narrow)]))
    for copy in narrow[-1:] + sum(wide, []) + narrow[:-1]:
        copy.start()
    lane = lax.broadcasted_iota(jnp.int32, (rows, HEAD_DIM), 1)
    square = (HEAD_DIM, HEAD_DIM)
    same = lax.broadcasted_iota(jnp.int32, square, 0) == lax.broadcasted_iota(jnp.int32, square, 1)
    identity = jnp.where(same, 1.0, 0.0).astype(BF16)
    ones = jnp.ones((2 * HEAD_DIM, HEAD_DIM), BF16)
    q_ref, o_ref, g_ref = wide_buf
    heads = width // HEAD_DIM
    for group in range(groups):
        for copy in wide[group]:
            copy.wait()
        for head in range(group * heads, (group + 1) * heads):
            cols = head_slice(head)
            span = slice(head * rows, (head + 1) * rows)
            g = g_ref[:, cols]
            product = g.astype(F32) * o_ref[:, cols].astype(F32)
            high = product.astype(BF16)
            low = (product - high.astype(F32)).astype(BF16)
            left = dot(jnp.concatenate([high, low], axis=1), ones)
            terms = jnp.zeros((rows, HEAD_DIM), F32)
            for term in range(DELTA_TERMS):
                rounded = left.astype(BF16).astype(F32)
                terms = jnp.where(lane == term, rounded, terms)
                left = left - rounded
            q_rows[span, :] = q_ref[:, cols]
            g_rows[span, :HEAD_DIM] = g
            g_rows[span, HEAD_DIM:] = terms.astype(BF16)
        span = slice(group * heads * rows, (group + 1) * heads * rows)
        q_cols[:, span] = dot(identity, q_rows[span, :], NT).astype(BF16)
        g_cols[:, span] = dot(identity, g_rows[span, :HEAD_DIM], NT).astype(BF16)
    for copy in narrow:
        copy.wait()
    length = len_ref[lax.axis_index("seq")]
    live_ref[...] = jnp.where(lax.broadcasted_iota(jnp.int32, live_ref.shape, 0) < length, 1.0, 0.0)


def prepare(lengths, q, o, g, rk, rv):
    rows, width = q.shape
    groups = rk.shape[1] // HEAD_DIM
    flat = rows * width // HEAD_DIM
    narrow = [rk, rv]
    return pl.pallas_call(
        functools.partial(prepare_kernel, groups),
        in_specs=[HBM_SPEC] * 6,
        out_specs=[VMEM_SPEC] * 7,
        out_shape=[
            shape(flat, HEAD_DIM),
            shape(flat, 2 * HEAD_DIM),
            shape(HEAD_DIM, flat),
            shape(HEAD_DIM, flat),
            jax.ShapeDtypeStruct((rows, HEAD_DIM), F32),
        ]
        + [shape(*x.shape) for x in narrow],
        scratch_shapes=[pltpu.VMEM((rows, width), BF16)] * 3
        + [pltpu.SMEM(lengths.shape, jnp.int32), pltpu.SemaphoreType.DMA((groups, 3)), pltpu.SemaphoreType.DMA((3,))],
        compiler_params=PARAMS,
        cost_estimate=pl.CostEstimate(flops=rows * width * 4000, bytes_accessed=16 * rows * width, transcendentals=0),
    )(*in_hbm(lengths, q, o, g, *narrow))


def read_pieces(joined, refs):
    k_refs, v_refs = [], []
    for both in joined:
        k_refs.append(refs[0].at[0] if both else refs[0])
        v_refs.append(refs[0].at[1] if both else refs[1])
        refs = refs[1 if both else 2 :]
    return k_refs, v_refs, refs


def attention_kernel(chips, piece_rows, joined, live_ref, q_rows, g_rows, q_cols, g_cols, rk_ref, rv_ref, *rest):
    pieces = CORES * chips
    k_refs, v_refs, rest = read_pieces(joined, rest)
    (ds_ref, drk_ref, drv_ref), rest = rest[:3], rest[3:]
    d_own, d_other, rest = rest[:chips], rest[chips : 2 * chips], rest[2 * chips :]
    k_buf, v_buf, s_buf, dp_buf, p_buf = rest
    rows, width = rk_ref.shape
    groups = width // HEAD_DIM
    block = q_rows.shape[0] // groups // 2
    keys = k_buf.shape[1]
    prompt = keys - rows
    diagonal = lax.broadcasted_iota(jnp.int32, (CHUNK, rows), 1) - lax.broadcasted_iota(jnp.int32, (CHUNK, rows), 0)
    minus = jnp.where(lax.broadcasted_iota(jnp.int32, (keys, HEAD_DIM), 1) < DELTA_TERMS, -1.0, 0.0).astype(BF16)

    def place(half):
        return slice(half * block, (half + 1) * block)

    def load_keys(group):
        cols = head_slice(group)
        for i in range(pieces):
            span = slice(i * piece_rows, (i + 1) * piece_rows)
            k_buf[group, span, :] = k_refs[i][:, cols]
            v_buf[group, span, :HEAD_DIM] = v_refs[i][:, cols]
        k_buf[group, prompt:, :] = rk_ref[:, cols]
        v_buf[group, prompt:, :HEAD_DIM] = rv_ref[:, cols]
        v_buf[group, :, HEAD_DIM:] = minus

    def scores(half):
        s_buf[half % 2] = dot(q_rows[place(half), :], k_buf[half // 2], NT)

    def prob_grads(half):
        dp_buf[half % 2] = dot(g_rows[place(half), :], v_buf[half // 2], NT)

    def soften(half, low):
        slot = half % 2
        first = low % rows
        span = slice(low, low + CHUNK)
        s = s_buf[slot, span, :]
        s = jnp.concatenate([s[:, :prompt], jnp.where(diagonal > first, -1e30, s[:, prompt:])], axis=1)
        e = jnp.exp2((s - jnp.max(s, axis=1, keepdims=True)) * (SCALE * LOG2E))
        weight = (1.0 / jnp.sum(e, axis=1, keepdims=True)) * live_ref[first : first + CHUNK, :]
        p = e * jnp.concatenate([weight] * (keys // HEAD_DIM), axis=1)
        p_buf[slot, span, :] = p.astype(BF16)
        ds_ref[half * block + low : half * block + low + CHUNK, :] = (p * dp_buf[slot, span, :]).astype(BF16)

    halves = 2 * groups
    held = None
    for half in range(-1, halves):
        if half + 1 < halves:
            if (half + 1) % 2 == 0:
                load_keys((half + 1) // 2)
            scores(half + 1)
            prob_grads(half + 1)
        if half < 0:
            continue
        for low in range(0, block, CHUNK):
            soften(half, low)
        dk = dot(q_cols[:, place(half)], ds_ref[place(half), :])
        dv = dot(g_cols[:, place(half)], p_buf[half % 2])
        if half % 2 == 0:
            held = (dk, dv)
            continue
        cols = head_slice(half // 2)
        dk = ((held[0] + dk) * SCALE).T
        dv = (held[1] + dv).T
        for kind, grad in enumerate((dk, dv)):
            for i in range(chips):
                d_own[i][kind, :, cols] = grad[i * piece_rows : (i + 1) * piece_rows]
                d_other[i][kind, :, cols] = grad[(chips + i) * piece_rows : (chips + i + 1) * piece_rows].astype(BF16)
        drk_ref[:, cols] = dk[prompt:].astype(BF16)
        drv_ref[:, cols] = dv[prompt:].astype(BF16)


def attention(prepared, kv_pieces):
    q_rows, g_rows, q_cols, g_cols, live, rk, rv = prepared
    rows, kv_width = rk.shape
    groups = kv_width // HEAD_DIM
    flat = q_rows.shape[0]
    pieces = len(kv_pieces)
    chips = pieces // CORES
    piece_rows = kv_pieces[0][0].shape[-2]
    joined = [len(piece) == 1 for piece in kv_pieces]
    flat_pieces = sum(kv_pieces, [])
    keys = pieces * piece_rows + rows
    block = flat // groups // 2
    return pl.pallas_call(
        functools.partial(attention_kernel, chips, piece_rows, joined),
        in_specs=[VMEM_SPEC] * (7 + len(flat_pieces)),
        out_specs=[VMEM_SPEC] * (3 + 2 * chips),
        out_shape=[shape(flat, keys), shape(rows, kv_width), shape(rows, kv_width)]
        + [jax.ShapeDtypeStruct((2, piece_rows, kv_width), F32)] * chips
        + [shape(2, piece_rows, kv_width)] * chips,
        scratch_shapes=[
            pltpu.VMEM((groups, keys, HEAD_DIM), BF16),
            pltpu.VMEM((groups, keys, 2 * HEAD_DIM), BF16),
            pltpu.VMEM((2, block, keys), F32),
            pltpu.VMEM((2, block, keys), F32),
            pltpu.VMEM((2, block, keys), BF16),
        ],
        compiler_params=PARAMS,
        cost_estimate=pl.CostEstimate(
            flops=10 * flat * keys * HEAD_DIM, bytes_accessed=10 * flat * HEAD_DIM, transcendentals=flat * keys
        ),
    )(live, q_rows, g_rows, q_cols, g_cols, rk, rv, *flat_pieces)


def query_grad_kernel(joined, ds_ref, rk_ref, drk_in, drv_in, *rest):
    k_refs, _, rest = read_pieces(joined, rest)
    (dq_out, drk_out, drv_out), (k_buf, dq_buf, wide_sem, narrow_sem) = rest[:3], rest[3:]
    rows, width = rk_ref.shape
    groups = width // HEAD_DIM
    flat = ds_ref.shape[0] // groups
    step = dq_buf.shape[1] // groups
    copies = [
        pltpu.make_async_copy(src, out, narrow_sem.at[i]) for i, (src, out) in enumerate(((drk_in, drk_out), (drv_in, drv_out)))
    ]
    for copy in copies:
        copy.start()
    for group in range(groups):
        low = 0
        for ref in k_refs + [rk_ref]:
            k_buf[group, low : low + ref.shape[0], :] = ref[:, head_slice(group)]
            low += ref.shape[0]
        dq = (dot(ds_ref[group * flat : (group + 1) * flat, :], k_buf[group]) * SCALE).astype(BF16)
        for i in range(flat // rows):
            dq_buf[:, head_slice(group * (flat // rows) + i)] = dq[i * rows : (i + 1) * rows]
        part = slice(group * step, (group + 1) * step)
        copies.append(pltpu.make_async_copy(dq_buf.at[:, part], dq_out.at[:, part], wide_sem.at[group]))
        copies[-1].start()
    for copy in copies:
        copy.wait()


def query_grads(ds, rk, drk, drv, kv_pieces):
    rows, kv_width = rk.shape
    flat, keys = ds.shape
    groups = kv_width // HEAD_DIM
    wide = (rows, flat // rows * HEAD_DIM)
    joined = [len(piece) == 1 for piece in kv_pieces]
    flat_pieces = sum(kv_pieces, [])
    return pl.pallas_call(
        functools.partial(query_grad_kernel, joined),
        in_specs=[VMEM_SPEC] * (4 + len(flat_pieces)),
        out_specs=[HBM_SPEC] * 3,
        out_shape=[shape(*wide), shape(rows, kv_width), shape(rows, kv_width)],
        scratch_shapes=[
            pltpu.VMEM((groups, keys, HEAD_DIM), BF16),
            pltpu.VMEM(wide, BF16),
            pltpu.SemaphoreType.DMA((groups,)),
            pltpu.SemaphoreType.DMA((2,)),
        ],
        compiler_params=PARAMS,
        cost_estimate=pl.CostEstimate(flops=4 * flat * keys * HEAD_DIM, bytes_accessed=4 * flat * keys, transcendentals=0),
    )(ds, rk, drk, drv, *flat_pieces)


def exchange(x, links):
    routes = [(a, b) for pair in links for a, b in (pair, pair[::-1])]
    pairs = [(CORES * a + core, CORES * b + core) for a, b in routes for core in range(CORES)]
    return lax.ppermute(x, "seq", pairs)


def chip_links(chips, step):
    return [(chip, chip ^ step) for chip in range(chips) if chip < chip ^ step]


def swap_core(x, chips):
    pairs = [(CORES * chip + core, CORES * chip + 1 - core) for chip in range(chips) for core in range(CORES)]
    return lax.ppermute(x, "seq", pairs)


def local(chips, queries, outputs, out_grads, resp_keys, resp_values, lengths, prompt_keys, prompt_values):
    steps = list(range(1, chips))
    raw = [prompt_keys, prompt_values]
    kind = lax.broadcasted_iota(jnp.int32, (2,) + prompt_keys.shape, 0)
    kv = [jnp.where(kind == 0, prompt_keys[None], prompt_values[None])]
    far = [[exchange(x, chip_links(chips, step)) for x in (raw if step == 2 else kv)] for step in steps]
    prepared = prepare(lengths, queries[0], outputs[0], out_grads[0], resp_keys[0], resp_values[0])
    live = prepared[4]
    far[1] = [lax.optimization_barrier((x, live))[0] for x in far[1]]
    first = [swap_core(x, chips) for x in far[1]]
    far = [piece if i == 1 else [lax.optimization_barrier((x, first))[0] for x in piece] for i, piece in enumerate(far)]
    own = [kv] + far
    other = [first if i == 2 else [swap_core(x, chips) for x in piece] for i, piece in enumerate(own)]
    ds, drk, drv, *grads = attention(prepared, own + other)
    both = [None] * chips
    for step in steps[1:2] + steps[:1] + steps[2:]:
        both[step] = grads[step] + swap_core(grads[chips + step], chips).astype(F32)
    sent = [x.astype(BF16) for x in both[1:]]
    home = lax.optimization_barrier((grads[chips], sent[-1]))[0]
    both[0] = grads[0] + swap_core(home, chips).astype(F32)
    back = [exchange(sent[step - 1], chip_links(chips, step)) for step in steps[1:2] + steps[:1] + steps[2:]]
    ds = lax.optimization_barrier((ds, [sent[step - 1] for step in steps[1:2] + steps[:1] + steps[2:]]))[0]
    dq, drk, drv = query_grads(ds, prepared[5], drk, drv, own + other)
    dq, back[0] = lax.optimization_barrier((dq, back[0]))
    total = sum([x.astype(F32) for x in back], both[0]).astype(BF16)
    return dq[None], drk[None], drv[None], total[0], total[1]


def solution(mesh):
    chips = mesh.shape["seq"] // CORES
    split = ("dp", "seq")
    row3 = P(split, None, None)
    row2 = P(split, None)
    return jax.shard_map(
        functools.partial(local, chips),
        mesh=mesh,
        in_specs=(row3, row3, row3, row3, row3, P("dp"), row2, row2),
        out_specs=(row3, row3, row3, row2, row2),
        check_vma=False,
    )
```
